32 devices in a mesh: blk: 8 (over z, x), head: 4 (over y, core).
Axes of the slice: x: 2, y: 2, z: 4, core: 2. Of those that a mesh axis runs over, the one named last changes fastest.
Arguments:
- inward: float32 [3, 2048, 2048], P(None, 'blk', 'head'), may hold values from -0.125 to 0.125
- outward: float32 [2048, 2048], P('head', 'blk'), may hold values from -6 to 6
- expand: float32 [2048, 8192], P('blk', 'head'), may hold values from -0.125 to 0.125
- contract: float32 [8192, 2048], P('head', 'blk'), may hold values from -0.0625 to 0.0625
- image_table: float32 [8192, 2048], P('blk', 'head'), may hold values from -0.75 to 0.75
- code_table: float32 [1280, 2048], P('blk', 'head'), may hold values from -0.75 to 0.75
- readout: float32 [2048, 8192], P('blk', 'head')
- gains: float32 [3, 2048], P(None, 'blk'), may hold values from 0.5 to 1.5
- inward_first: float32 [3, 2048, 2048], P(None, 'blk', 'head'), may hold values from -6.67572e-06 to 6.67572e-06
- outward_first: float32 [2048, 2048], P('head', 'blk'), may hold values from -3.5762787e-07 to 3.5762787e-07
- expand_first: float32 [2048, 8192], P('blk', 'head'), may hold values from -1.4305115e-06 to 1.4305115e-06
- contract_first: float32 [8192, 2048], P('head', 'blk'), may hold values from -1.4305115e-06 to 1.4305115e-06
- image_first: float32 [8192, 2048], P('blk', 'head'), may hold values from -3.33786e-06 to 3.33786e-06
- code_first: float32 [1280, 2048], P('blk', 'head'), may hold values from -4.7683716e-06 to 4.7683716e-06
- readout_first: float32 [2048, 8192], P('blk', 'head'), may hold values from -3.8146973e-06 to 3.8146973e-06
- gains_first: float32 [3, 2048], P(None, 'blk'), may hold values from -1.335144e-05 to 1.335144e-05
- inward_second: float32 [3, 2048, 2048], P(None, 'blk', 'head'), may hold values from 8.1857047e-13 to 3.2742819e-12
- outward_second: float32 [2048, 2048], P('head', 'blk'), may hold values from 2.4318695e-15 to 9.7036365e-15
- expand_second: float32 [2048, 8192], P('blk', 'head'), may hold values from 4.053116e-14 to 1.6212464e-13
- contract_second: float32 [8192, 2048], P('head', 'blk'), may hold values from 3.618002e-14 to 1.4483929e-13
- image_second: float32 [8192, 2048], P('blk', 'head'), may hold values from 2.002716e-13 to 8.010864e-13
- code_second: float32 [1280, 2048], P('blk', 'head'), may hold values from 4.997253e-13 to 2.0027161e-12
- readout_second: float32 [2048, 8192], P('blk', 'head'), may hold values from 3.1292438e-13 to 1.2516975e-12
- gains_second: float32 [3, 2048], P(None, 'blk'), may hold values from 3.076172e-12 to 1.2304688e-11
- token_ids: int32 [2, 2048], P(None, 'blk'), may hold values from 0 to 8191, as said below
- modality: int32 [2, 2048], P(None, 'blk'), may hold values from 0 to 2
- clip_lengths: int32 [2], replicated, may hold values from 1024 to 2048, as said below
- loss_mask: int32 [2, 2048], P(None, 'blk'), may hold values from 0 to 1
- targets: int32 [2, 2048], P(None, 'blk'), may hold values from 0 to 8191
Outputs:
- inward_next: float32 [3, 2048, 2048], P(None, 'blk', 'head')
- inward_first_next: float32 [3, 2048, 2048], P(None, 'blk', 'head')
- inward_second_next: float32 [3, 2048, 2048], P(None, 'blk', 'head')
- outward_next: float32 [2048, 2048], P('head', 'blk')
- outward_first_next: float32 [2048, 2048], P('head', 'blk')
- outward_second_next: float32 [2048, 2048], P('head', 'blk')
- expand_next: float32 [2048, 8192], P('blk', 'head')
- expand_first_next: float32 [2048, 8192], P('blk', 'head')
- expand_second_next: float32 [2048, 8192], P('blk', 'head')
- contract_next: float32 [8192, 2048], P('head', 'blk')
- contract_first_next: float32 [8192, 2048], P('head', 'blk')
- contract_second_next: float32 [8192, 2048], P('head', 'blk')
- image_next: float32 [8192, 2048], P('blk', 'head')
- image_first_next: float32 [8192, 2048], P('blk', 'head')
- image_second_next: float32 [8192, 2048], P('blk', 'head')
- code_next: float32 [1280, 2048], P('blk', 'head')
- code_first_next: float32 [1280, 2048], P('blk', 'head')
- code_second_next: float32 [1280, 2048], P('blk', 'head')
- readout_next: float32 [2048, 8192], P('blk', 'head')
- readout_first_next: float32 [2048, 8192], P('blk', 'head')
- readout_second_next: float32 [2048, 8192], P('blk', 'head')
- gains_next: float32 [3, 2048], P(None, 'blk')
- gains_first_next: float32 [3, 2048], P(None, 'blk')
- gains_second_next: float32 [3, 2048], P(None, 'blk')
- loss_sum: float32 [], replicated
- loss_count: float32 [], replicated
- grad_norm: float32 [], replicated
The draws below stay inside these ranges and needn't reach their ends.
Inputs may be any that keep to these rules, and one draw needn't show every extreme that they name: `token_ids`: ids are below 8192 at image positions, below 1024 at text positions and below 256 at action positions. `clip_lengths`: at least one clip uses all 2048 positions.
All inputs are finite; a program needn't handle non-finite values.
Results may differ from the reference program's by a relative error of at most 0.03.
Values may be sent and summed in bfloat16 or wider, within the bound.
No kernel may reach another device: no remote copies, remote signals or barrier semaphores. Data moves between devices by JAX's collectives and lax.ppermute only.
A program may use at most 256 MiB of HBM per device.

```python
import math
import jax
import jax.numpy as jnp
import numpy as np
from jax import lax

D = 2048
HEADS = 16
HD = 128
FF = 8192
VI = 8192
VT = 1024
VA = 256
CLIPS = 2
STEP = 10
LEN = 2048


def token_pair(key):
    kinds = jax.random.randint(jax.random.fold_in(key, 11), (CLIPS, LEN), 0, 10)
    modal = jnp.where(kinds < 7, 0, jnp.where(kinds < 9, 1, 2))
    raw = jax.random.randint(jax.random.fold_in(key, 12), (CLIPS, LEN), 0, VI)
    ids = jnp.where(modal == 0, raw, jnp.where(modal == 1, raw % VT, raw % VA))
    return (ids.astype(jnp.int32), modal.astype(jnp.int32))


def draw_token_ids(key, part):
    ids, modal = token_pair(key)
    return ids


def draw_modality(key, part):
    ids, modal = token_pair(key)
    return modal


def draw_clip_lengths(key, part):
    key = jax.random.fold_in(key, 3)
    full = jax.random.randint(jax.random.fold_in(key, 1), (), 0, CLIPS)
    other = jax.random.randint(jax.random.fold_in(key, 2), (CLIPS,), LEN // 2, LEN + 1)
    return jnp.where(jnp.arange(CLIPS) == full, LEN, other).astype(jnp.int32)


def draw_loss_mask(key, part):
    key = jax.random.fold_in(key, 4)
    rolls = jax.random.randint(key, (CLIPS, LEN), 0, 4 * LEN)
    places = jnp.arange(LEN)[None, :]
    return (rolls < LEN + 2 * places).astype(jnp.int32)


def draw_readout(key, part):
    key = jax.random.fold_in(key, 5)
    column = jnp.arange(VI).astype(jnp.float32) / (VI - 1)
    base = jax.random.normal(key, (D, VI), jnp.float32)
    spread = 1.0 + 2.0 * column
    return base * spread[None, :] * D ** (-0.5)


def plant(values, own_key, least, high):
    extent = values.shape
    index_at = [jax.random.randint(jax.random.fold_in(own_key, axis), (), 0, extent[axis]) for axis in range(len(extent))]
    values = values.at[tuple(index_at)].set(least)
    longest = extent.index(max(extent))
    index_at[longest] = (index_at[longest] + 1) % extent[longest]
    return values.at[tuple(index_at)].set(high)


def level_of(own_key, dims, pieces, least, largest):
    level, own = 1.0, jax.random.fold_in(own_key, 6)
    for axis_at, parts in pieces:
        steps = jnp.exp(jax.random.uniform(jax.random.fold_in(own, axis_at), (parts,), jnp.float32, least / len(pieces), largest / len(pieces)))
        level = level * jnp.repeat(steps, dims[axis_at] // parts).reshape([-1 if axis == axis_at else 1 for axis in range(len(dims))])
    return level


def rank_bounds(number_of, lean):
    weights = [(1 << 20) // math.isqrt(rank ** lean) + 1 for rank in range(1, number_of + 1)]
    scale = 1 + sum(weights) // (1 << 30)
    return np.cumsum(np.array([max(1, weight // scale) for weight in weights]))


def skewed_ids(rng, shape, count, lean):
    table = rank_bounds(count, lean)
    lot = jax.random.randint(jax.random.fold_in(rng, 1), shape, 0, int(table[count - 1]))
    rank = jnp.searchsorted(jnp.asarray(table, jnp.int32), lot, side="right")
    return jax.random.permutation(jax.random.fold_in(rng, 2), count)[rank].astype(jnp.int32)


def centred(own_key, extent, scale, bound, cuts=(), held_as=jnp.bfloat16):
    values = jax.random.normal(own_key, extent, jnp.float32) * scale
    if len(cuts) > 0:
        values = level_of(own_key, extent, cuts, -0.22, 0.18) * values
    return jnp.clip(values, min=-bound, max=bound).astype(held_as)


def setup_inputs(seed: int = 0) -> dict:
    keys = jax.random.split(jax.random.key(seed), 30)
    return {
        "inward": centred(keys[0], (3, D, D), D ** -0.5, 0.125, ((1, 8), (2, 4)), jnp.float32),
        "outward": centred(keys[1], (D, D), ((LEN // 2) ** 0.5 * D ** -0.5), 6.0, ((0, 4), (1, 8)), jnp.float32),
        "expand": centred(keys[2], (D, FF), D ** -0.5, 0.125, ((0, 8), (1, 4)), jnp.float32),
        "contract": centred(keys[3], (FF, D), FF ** -0.5, 0.0625, ((0, 4), (1, 8)), jnp.float32),
        "image_table": centred(keys[4], (VI, D), 0.05, 0.75, ((0, 8), (1, 4)), jnp.float32),
        "code_table": centred(keys[5], (VT + VA, D), 0.05, 0.75, ((0, 8), (1, 4)), jnp.float32),
        "readout": draw_readout(jax.random.fold_in(keys[29], 71), 0),
        "gains": jnp.clip(1.0 + 0.1 * jax.random.normal(keys[7], (3, D), jnp.float32), 0.5, 1.5),
        "inward_first": centred(keys[8], (3, D, D), (0.00155 * (3 * D * D) ** -0.5), 6.67572021484375e-06, ((1, 8), (2, 4)), jnp.float32),
        "outward_first": centred(keys[9], (D, D), (0.000049 * (D * D) ** -0.5), 3.5762786865234375e-07, ((0, 4), (1, 8)), jnp.float32),
        "expand_first": centred(keys[10], (D, FF), (0.0004 * (D * FF) ** -0.5), 1.430511474609375e-06, ((0, 8), (1, 4)), jnp.float32),
        "contract_first": centred(keys[11], (FF, D), (0.000377 * (FF * D) ** -0.5), 1.430511474609375e-06, ((0, 4), (1, 8)), jnp.float32),
        "image_first": centred(keys[12], (VI, D), (0.000888 * (VI * D) ** -0.5), 3.337860107421875e-06, ((0, 8), (1, 4)), jnp.float32),
        "code_first": centred(keys[13], (VT + VA, D), (0.000555 * ((VT + VA) * D) ** -0.5), 4.76837158203125e-06, ((0, 8), (1, 4)), jnp.float32),
        "readout_first": centred(keys[14], (D, VI), (0.00111 * (D * VI) ** -0.5), 3.814697265625e-06, ((0, 8), (1, 4)), jnp.float32),
        "gains_first": centred(keys[15], (3, D), (0.0000666 * (3 * D) ** -0.5), 1.33514404296875e-05, ((1, 8),), jnp.float32),
        "inward_second": jnp.clip(jnp.exp(math.log(3.2742818872888435e-12) - 1.3862944 * jax.random.uniform(keys[16], (3, D, D), jnp.float32) ** level_of(keys[16], (3, D, D), ((1, 8), (2, 4)), -0.2, 0.2)), 8.185704718222109e-13, 3.2742818872888435e-12),
        "outward_second": jnp.clip(jnp.exp(math.log(9.703636548799577e-15) - 1.3838404 * jax.random.uniform(keys[17], (D, D), jnp.float32) ** level_of(keys[17], (D, D), ((0, 4), (1, 8)), -0.2, 0.2)), 2.431869496291486e-15, 9.703636548799577e-15),
        "expand_second": jnp.clip(jnp.exp(math.log(1.6212464042705127e-13) - 1.3862944 * jax.random.uniform(keys[18], (D, FF), jnp.float32) ** level_of(keys[18], (D, FF), ((0, 8), (1, 4)), -0.2, 0.2)), 4.053116010676282e-14, 1.6212464042705127e-13),
        "contract_second": jnp.clip(jnp.exp(math.log(1.448392865062778e-13) - 1.3871177 * jax.random.uniform(keys[19], (FF, D), jnp.float32) ** level_of(keys[19], (FF, D), ((0, 4), (1, 8)), -0.2, 0.2)), 3.618001961935326e-14, 1.448392865062778e-13),
        "image_second": jnp.clip(jnp.exp(math.log(8.010864107482751e-13) - 1.3862944 * jax.random.uniform(keys[20], (VI, D), jnp.float32) ** level_of(keys[20], (VI, D), ((0, 8), (1, 4)), -0.2, 0.2)), 2.0027160268706878e-13, 8.010864107482751e-13),
        "code_second": jnp.clip(jnp.exp(math.log(2.002716135290905e-12) - 1.388201 * jax.random.uniform(keys[21], (VT + VA, D), jnp.float32) ** level_of(keys[21], (VT + VA, D), ((0, 8), (1, 4)), -0.2, 0.2)), 4.997253153816994e-13, 2.002716135290905e-12),
        "readout_second": jnp.clip(jnp.exp(math.log(1.251697530346707e-12) - 1.3862944 * jax.random.uniform(keys[22], (D, VI), jnp.float32) ** level_of(keys[22], (D, VI), ((0, 8), (1, 4)), -0.2, 0.2)), 3.1292438258667676e-13, 1.251697530346707e-12),
        "gains_second": jnp.clip(jnp.exp(math.log(1.230468765073267e-11) - 1.3862944 * jax.random.uniform(keys[23], (3, D), jnp.float32) ** level_of(keys[23], (3, D), ((1, 8),), -0.2, 0.2)), 3.0761719126831677e-12, 1.230468765073267e-11),
        "token_ids": draw_token_ids(jax.random.fold_in(keys[29], 71), 0),
        "modality": draw_modality(jax.random.fold_in(keys[29], 71), 0),
        "clip_lengths": draw_clip_lengths(jax.random.fold_in(keys[29], 71), 0),
        "loss_mask": draw_loss_mask(jax.random.fold_in(keys[29], 71), 0),
        "targets": plant(skewed_ids(keys[28], (CLIPS, LEN), VI, 0), jax.random.fold_in(keys[28], 3), 0, VI - 1).astype(jnp.int32),
    }


EPS = 1e-05
ZCOEF = 0.01
CLIP = 0.02
BETA1 = 0.9
BETA2 = 0.95
ADAM_EPS = 1e-08
DECAY = 0.1
RATE_FACTOR = 1.5
GAIN_RATE = 0.8
HIGH = lax.Precision.HIGHEST

@jax.custom_vjp
def low(v):
    return lax.optimization_barrier(v.astype(jnp.bfloat16)).astype(jnp.float32)

@jax.custom_vjp
def low_back(v):
    return v

def low_keep(v):
    return (low(v), None)

def low_pass(kept, grad):
    return (grad,)

def back_keep(v):
    return (v, None)

def back_low(kept, grad):
    return (low(grad),)
low.defvjp(low_keep, low_pass)
low_back.defvjp(back_keep, back_low)

def rms_norm(hidden, gain):
    return hidden * lax.rsqrt(lax.optimization_barrier(jnp.mean(hidden * hidden, axis=-1, keepdims=True)) + EPS) * gain

def attention(queries, keys_all, values_all):
    scale = HD ** (-0.5)
    block = min(512, LEN)
    blocks = LEN // block
    key_pos = jnp.arange(LEN).astype(jnp.int32)

    def one_block(start):
        chosen = lax.dynamic_slice_in_dim(queries, start, block, 1)
        raw = jnp.einsum('cqhd,ckhd->chqk', chosen, keys_all, precision=HIGH)
        scores = low_back(scale * raw)
        query_pos = start + jnp.arange(block).astype(jnp.int32)
        seen = key_pos[None, :] <= query_pos[:, None]
        scores = jnp.where(seen, scores, -1e+30)
        probs = low(jax.nn.softmax(scores, axis=-1))
        return jnp.einsum('chqk,ckhd->cqhd', probs, values_all, precision=HIGH)
    starts = (jnp.arange(blocks) * block).astype(jnp.int32)
    outputs = lax.map(jax.checkpoint(one_block), starts)
    return jnp.moveaxis(outputs, 0, 1).reshape(CLIPS, LEN, D)

def forward(weights, token_ids, modality, targets, weight_of):
    inward, outward, expand, contract, image_table, code_table, readout, gains = weights
    inward, outward, expand, contract = (low(inward), low(outward), low(expand), low(contract))
    image_table, code_table, readout = (low(image_table), low(code_table), low(readout))
    code_rows = jnp.clip(jnp.where(modality == 1, token_ids, VT + token_ids), 0, VT + VA - 1)
    embedded = jnp.where((modality == 0)[..., None], image_table[token_ids], code_table[code_rows])
    normed = low(rms_norm(embedded, gains[0]))
    mixed = low(low_back(jnp.einsum('ctd,sde->scte', normed, inward, precision=HIGH)))
    queries = mixed[0].reshape(CLIPS, LEN, HEADS, HD)
    keys_all = mixed[1].reshape(CLIPS, LEN, HEADS, HD)
    values_all = mixed[2].reshape(CLIPS, LEN, HEADS, HD)
    heads_out = low(low_back(attention(queries, keys_all, values_all)))
    first = embedded + low_back(jnp.einsum('cte,ed->ctd', heads_out, outward, precision=HIGH))
    normed_mid = low(rms_norm(first, gains[1]))
    hidden_up = low_back(jnp.einsum('ctd,df->ctf', normed_mid, expand, precision=HIGH))
    active = low(jax.nn.gelu(hidden_up))
    second = first + low_back(jnp.einsum('ctf,fd->ctd', active, contract, precision=HIGH))
    final_in = low(rms_norm(second, gains[2]))
    logits = low_back(jnp.einsum('ctd,dv->ctv', final_in, readout, precision=HIGH))
    log_norm = jax.nn.logsumexp(logits, axis=-1)
    picked = jnp.take_along_axis(logits, targets[..., None], axis=-1)[..., 0]
    per_token = (log_norm - picked + ZCOEF * log_norm * log_norm) * weight_of
    total = jnp.sum(per_token)
    count = jnp.sum(weight_of)
    return (total / count, (total, count))

def adamw(weight, first, second, grad, rate, decay):
    first = BETA1 * first + (1.0 - BETA1) * grad
    second = BETA2 * second + (1.0 - BETA2) * grad * grad
    first_hat = first / (1.0 - BETA1 ** STEP)
    second_hat = second / (1.0 - BETA2 ** STEP)
    weight = weight - rate * (first_hat / (jnp.sqrt(second_hat) + ADAM_EPS) + decay * weight)
    return (weight, first, second)

def reference(inward, outward, expand, contract, image_table, code_table, readout, gains, inward_first, outward_first, expand_first, contract_first, image_first, code_first, readout_first, gains_first, inward_second, outward_second, expand_second, contract_second, image_second, code_second, readout_second, gains_second, token_ids, modality, clip_lengths, loss_mask, targets):
    weights = (inward, outward, expand, contract, image_table, code_table, readout, gains)
    firsts = (inward_first, outward_first, expand_first, contract_first, image_first, code_first, readout_first, gains_first)
    seconds = (inward_second, outward_second, expand_second, contract_second, image_second, code_second, readout_second, gains_second)
    places = jnp.arange(LEN).astype(jnp.int32)
    weight_of = ((loss_mask == 1) & (places[None, :] < clip_lengths[:, None])).astype(jnp.float32)

    def objective(params):
        return forward(params, token_ids, modality, targets, weight_of)
    mean_loss, pullback, totals = jax.vjp(objective, weights, has_aux=True)
    grads = pullback(jnp.ones_like(mean_loss))[0]
    squares = jnp.float32(0.0)
    for grad in grads:
        squares = squares + jnp.sum(grad * grad)
    grad_norm = jnp.sqrt(squares)
    factor = jnp.minimum(1.0, CLIP / grad_norm)
    spreads = [D ** (-0.5), (LEN // 2) ** 0.5 * D ** (-0.5), D ** (-0.5), FF ** (-0.5), 0.05, 0.05, 2.0 * D ** (-0.5)]
    result = []
    for index in range(8):
        rate = GAIN_RATE if index == 7 else RATE_FACTOR * spreads[index]
        decay = 0.0 if index == 7 else DECAY
        result.append(adamw(weights[index], firsts[index], seconds[index], grads[index] * factor, rate, decay))
    return (result[0][0], result[0][1], result[0][2], result[1][0], result[1][1], result[1][2], result[2][0], result[2][1], result[2][2], result[3][0], result[3][1], result[3][2], result[4][0], result[4][1], result[4][2], result[5][0], result[5][1], result[5][2], result[6][0], result[6][1], result[6][2], result[7][0], result[7][1], result[7][2], totals[0], totals[1], grad_norm)
```

```python
import jax
import jax.numpy as jnp
from jax import lax
from jax.sharding import PartitionSpec as P

D = 2048
HD = 128
FF = 8192
VT = 1024
VA = 256
STEP = 10


EPS = 1e-05
ZCOEF = 0.01
CLIP = 0.02
BETA1 = 0.9
BETA2 = 0.95
ADAM_EPS = 1e-08
DECAY = 0.1
RATE_FACTOR = 1.5
GAIN_RATE = 0.8

HALF = jnp.bfloat16
F32 = jnp.float32
NEG = -1e30
PAIR = 2


def flip(value, bit):
    count = lax.axis_size("blk")
    return lax.ppermute(value, "blk", [(i, i ^ bit) for i in range(count)])


def rms_norm(hidden, gain):
    return hidden * lax.rsqrt(jnp.mean(hidden * hidden, axis=-1, keepdims=True) + EPS) * gain


def norm_back(hidden, gain, upstream):
    unused, pullback = jax.vjp(rms_norm, hidden, gain)
    return pullback(upstream)


def dot(left, right, dims, out=F32):
    return lax.dot_general(left, right, (dims, ((), ())), preferred_element_type=F32).astype(out)


def adamw(weight, first, second, grad, rate, decay):
    first = BETA1 * first + (1.0 - BETA1) * grad
    second = BETA2 * second + (1.0 - BETA2) * grad * grad
    first_hat = first / (1.0 - BETA1**STEP)
    second_hat = second / (1.0 - BETA2**STEP)
    weight = weight - rate * (first_hat / (jnp.sqrt(second_hat) + ADAM_EPS) + decay * weight)
    return (weight, first, second)


def visible(query_pos, key_pos):
    return (key_pos[None, :] <= query_pos[:, None]) & (key_pos[None, :] >= 0)


def scores_of(queries, keys):
    return HD ** (-0.5) * jnp.einsum("qhd,khd->hqk", queries, keys, preferred_element_type=F32)


def attend(queries, keys, values, query_pos, key_pos, running):
    top_now, total_now, summed = running
    seen = visible(query_pos, key_pos)
    scores = jnp.where(seen, scores_of(queries, keys), NEG)
    top_next = jnp.maximum(top_now, jnp.max(scores, axis=-1))
    weights = jnp.where(seen, jnp.exp(scores - top_next[..., None]), 0.0)
    fading = jnp.exp(top_now - top_next)
    total_next = total_now * fading + jnp.sum(weights, axis=-1)
    summed = summed * fading[..., None] + jnp.einsum(
        "hqk,khd->hqd", weights.astype(HALF), values, preferred_element_type=F32
    )
    return (top_next, total_next, summed)


def attend_back(queries, keys, values, query_pos, key_pos, grad_out, log_total, inner):
    seen = visible(query_pos, key_pos)
    probs = jnp.where(seen, jnp.exp(scores_of(queries, keys) - log_total[..., None]), 0.0)
    grad_values = jnp.einsum(
        "hqk,qhd->khd", probs.astype(HALF), grad_out, preferred_element_type=F32
    )
    grad_probs = jnp.einsum("qhd,khd->hqk", grad_out, values, preferred_element_type=F32)
    grad_scores = (probs * (grad_probs - inner[..., None])).astype(HALF)
    grad_query = HD ** (-0.5) * jnp.einsum(
        "hqk,khd->qhd", grad_scores, keys, preferred_element_type=F32
    )
    grad_keys = HD ** (-0.5) * jnp.einsum(
        "hqk,qhd->khd", grad_scores, queries, preferred_element_type=F32
    )
    return (grad_query, grad_keys, grad_values)


def shards(
    inward,
    outward,
    expand,
    contract,
    image_table,
    code_table,
    readout,
    gains,
    inward_first,
    outward_first,
    expand_first,
    contract_first,
    image_first,
    code_first,
    readout_first,
    gains_first,
    inward_second,
    outward_second,
    expand_second,
    contract_second,
    image_second,
    code_second,
    readout_second,
    gains_second,
    token_ids,
    modality,
    clip_lengths,
    loss_mask,
    targets,
):
    blocks = lax.axis_size("blk")
    heads = lax.axis_size("head")
    blk = lax.axis_index("blk")
    head = lax.axis_index("head")
    clips, span = token_ids.shape
    length = span * blocks
    rows = D // blocks
    low = blk % 2
    side = (blk // 2) % 2
    high = blk // 4
    highs = blocks // 4
    groups = blocks // 2
    group = high * 2 + low
    per_clip = groups // clips
    clip = group // per_clip
    place = group % per_clip
    ranks = 2 * heads
    rank = side * heads + head
    team = clips * length // groups
    own = team // ranks
    high_bits = [1 << k for k in range(2, blocks.bit_length() - 1)]
    all_bits = [1, 2] + high_bits
    teams = [
        [i * heads + h for i in (base, base + PAIR) for h in range(heads)]
        for base in range(blocks)
        if not base & PAIR
    ]
    both = ("blk", "head")

    def gathered(block):
        return lax.all_gather(block, both, axis=0, tiled=True, axis_index_groups=teams)

    def reduced(partial):
        return lax.psum_scatter(
            partial, both, scatter_dimension=0, tiled=True, axis_index_groups=teams
        ).astype(F32)

    def index_of(shift):
        pairs = []
        for i in range(blocks):
            g = (i // 4) * 2 + i % 2
            far = g + shift
            if 0 <= far < groups and far // per_clip == g // per_clip:
                pairs.append((i, (far // 2) * 4 + (i & PAIR) + far % 2))
        return pairs

    small = jnp.concatenate(
        [part.astype(F32).reshape(-1) for part in (token_ids, modality, loss_mask, targets, gains)]
    )[None]
    for bit in all_bits:
        small = jnp.concatenate([small, flip(small, bit)])
    order = blk ^ jnp.arange(blocks)
    small = small[order]
    cells = clips * span
    ids_all, modality_all, mask_all, targets_all = (
        small[:, k * cells : (k + 1) * cells]
        .astype(jnp.int32)
        .reshape(blocks, clips, span)
        .transpose(1, 0, 2)
        .reshape(clips, length)
        for k in range(4)
    )
    gains_full = small[:, 4 * cells :].reshape(blocks, 3, rows).transpose(1, 0, 2).reshape(3, D)

    def sided(weight):
        return weight.astype(HALF).reshape(rows, 2, -1)

    qkv_local = inward.astype(HALF).reshape(3, rows, 2, -1).transpose(1, 2, 0, 3)
    local = [
        jnp.concatenate(
            [qkv_local.reshape(rows, 2, -1), sided(outward.astype(HALF).T)], axis=-1
        ),
        sided(expand),
        sided(contract.astype(HALF).T),
        sided(readout),
    ]

    def gathered_weight(halves):
        keep = lax.dynamic_index_in_dim(halves, side, 1, keepdims=False)
        send = lax.dynamic_index_in_dim(halves, 1 - side, 1, keepdims=False)
        came = flip(send, PAIR)
        mine = jnp.where(side == 0, jnp.stack([keep, came]), jnp.stack([came, keep]))
        pieces = {0: mine}
        for bit in high_bits + [1]:
            for mask in list(pieces):
                pieces[mask | bit] = flip(pieces[mask], bit)
        columns = mine.shape[-1]
        whole = jnp.zeros((highs, 2, 2, rows, columns), HALF)
        for mask, piece in pieces.items():
            whole = lax.dynamic_update_slice(
                whole,
                piece[None, :, None],
                (high ^ (mask >> 2), 0, low ^ (mask & 1), 0, 0),
            )
        return whole.reshape(D, columns)

    w_first, w_up, w_down, w_read = [gathered_weight(part) for part in local]
    head_columns = w_first.shape[-1] // 4
    w_in, w_out = w_first[:, : 3 * head_columns], w_first[:, 3 * head_columns :]
    local_heads = head_columns // HD

    def by_device(array):
        split = array.reshape(highs, 2, 2, team // 2)
        return split.transpose(0, 2, 1, 3).reshape(blocks, team // 2)

    image_rows = image_table.shape[0]
    code_local = code_table.shape[0]
    table = jnp.concatenate([image_table.astype(HALF), code_table.astype(HALF)])
    ids_dev, modality_dev = by_device(ids_all)[order], by_device(modality_all)[order]
    code_rows = jnp.clip(jnp.where(modality_dev == 1, ids_dev, VT + ids_dev), 0, VT + VA - 1)
    image_at = ids_dev - blk * image_rows
    code_at = code_rows - blk * code_local
    image_at = jnp.where((image_at >= 0) & (image_at < image_rows), image_at, -1)
    code_at = jnp.where((code_at >= 0) & (code_at < code_local), code_at + image_rows, -1)
    table_at = jnp.where(modality_dev == 0, image_at, code_at)
    table_rows = image_rows + code_local
    pick = (table_at.reshape(-1)[:, None] == jnp.arange(table_rows)[None, :]).astype(HALF)
    picked = dot(pick, table, ((1,), (0,)), HALF)
    width = table.shape[1]
    levels = len(all_bits)
    picked = picked.reshape((2,) * levels + (team // 2, width))

    def token_sum(part, bits):
        left = sorted(all_bits, reverse=True)
        for bit in bits:
            axis = left.index(bit)
            left.remove(bit)
            keep = lax.index_in_dim(part, 0, axis, keepdims=False)
            send = lax.index_in_dim(part, 1, axis, keepdims=False)
            part = keep + flip(send, bit)
        return part

    bits_a = [1, 2] + high_bits[::-1]
    bits_b = [2, 1] + high_bits[::-1]
    mid = width // 2
    block = jnp.concatenate(
        [token_sum(picked[..., :mid], bits_a), token_sum(picked[..., mid:], bits_b)], axis=-1
    )
    embedded = (
        gathered(block)
        .reshape(2, heads, team // 2, width)
        .transpose(0, 2, 1, 3)
        .reshape(team, heads * width)
    )
    embedded_own = lax.dynamic_slice_in_dim(embedded, rank * own, own, 0).astype(F32)

    normed_in = rms_norm(embedded.astype(F32), gains_full[0]).astype(HALF)
    mixed = dot(normed_in, w_in, ((1,), (0,)), HALF)
    queries, keys_own, values_own = (
        mixed[:, k * head_columns : (k + 1) * head_columns].reshape(team, local_heads, HD)
        for k in range(3)
    )
    offsets = jnp.arange(team)
    query_pos = place * team + offsets
    running = (
        jnp.full((local_heads, team), NEG, F32),
        jnp.zeros((local_heads, team), F32),
        jnp.zeros((local_heads, team, HD), F32),
    )
    earlier = []
    for back in range(1, per_clip):
        earlier.append(lax.ppermute((keys_own, values_own), "blk", index_of(back)))
    running = attend(queries, keys_own, values_own, query_pos, query_pos, running)
    for back in range(1, per_clip):
        keys_now, values_now = earlier[back - 1]
        running = attend(
            queries, keys_now, values_now, query_pos, query_pos - back * team, running
        )
    top_all, total_all, summed = running
    log_total = top_all + jnp.log(total_all)
    attn_heads = (summed / total_all[..., None]).transpose(1, 0, 2).astype(HALF)
    flat_heads = attn_heads.reshape(team, head_columns)
    first = embedded_own + reduced(dot(flat_heads, w_out, ((1,), (1,)), HALF))
    normed_mid = gathered(rms_norm(first, gains_full[1]).astype(HALF))
    hidden_up = dot(normed_mid, w_up, ((1,), (0,)))
    active = jax.nn.gelu(hidden_up).astype(HALF)
    second = first + reduced(dot(active, w_down, ((1,), (1,)), HALF))
    final_in = gathered(rms_norm(second, gains_full[2]).astype(HALF))
    logits = dot(final_in, w_read, ((1,), (0,)))

    def of_team(array):
        return lax.dynamic_slice(array, (clip, place * team), (1, team))[0]

    weight_all = (
        (mask_all == 1) & (jnp.arange(length)[None, :] < clip_lengths[:, None])
    ).astype(F32)
    loss_count = jnp.sum(weight_all)
    weight_of = of_team(weight_all)
    targets_own = of_team(targets_all)
    vocab_local = logits.shape[1]
    column_ids = (head * 2 + side) * vocab_local + jnp.arange(vocab_local)
    match = column_ids[None, :] == targets_own[:, None]
    top_vocab = jnp.max(logits, axis=-1)
    sum_vocab = jnp.sum(jnp.exp(logits - top_vocab[:, None]), axis=-1)
    hit_vocab = jnp.sum(jnp.where(match, logits, 0.0), axis=-1)
    stats = jnp.stack([top_vocab, sum_vocab, hit_vocab])
    steps = [("blk", PAIR)] + [("head", 1 << k) for k in range(heads.bit_length() - 1)]
    for axis, bit in steps:
        pairs = [(i, i ^ bit) for i in range(lax.axis_size(axis))]
        other = lax.ppermute(stats, axis, pairs)
        top = jnp.maximum(stats[0], other[0])
        total = stats[1] * jnp.exp(stats[0] - top) + other[1] * jnp.exp(other[0] - top)
        stats = jnp.stack([top, total, stats[2] + other[2]])
    log_norm = stats[0] + jnp.log(stats[1])
    per_token = (log_norm + ZCOEF * log_norm * log_norm - stats[2]) * weight_of
    loss_part = jnp.sum(per_token) * (rank == 0).astype(F32)

    token_grad = weight_of / loss_count
    probs = jnp.exp(logits - log_norm[:, None])
    grad_logits = (
        token_grad[:, None]
        * (probs * (1.0 + 2.0 * ZCOEF * log_norm)[:, None] - match.astype(F32))
    ).astype(HALF)

    def weight_grad(left, right):
        split = left.reshape(team, highs, 2, 2, rows)

        def part(at):
            chosen = lax.dynamic_index_in_dim(split, at, 3, keepdims=False)
            made = dot(chosen.reshape(team, highs * 2 * rows), right, ((0,), (0,)))
            return made.reshape((2,) * len(high_bits) + (2, rows, right.shape[1]))

        came = flip(part(1 - low).astype(HALF), 1)
        total = part(low) + came.astype(F32)
        for bit in high_bits[::-1]:
            at = (blk // bit) % 2
            send = lax.dynamic_index_in_dim(total, 1 - at, 0, keepdims=False)
            keep = lax.dynamic_index_in_dim(total, at, 0, keepdims=False)
            total = keep + flip(send.astype(HALF), bit).astype(F32)
        send = lax.dynamic_index_in_dim(total, 1 - side, 0, keepdims=False)
        keep = lax.dynamic_index_in_dim(total, side, 0, keepdims=False)
        came = flip(send.astype(HALF), PAIR).astype(F32)
        return jnp.where(
            side == 0, jnp.stack([keep, came], axis=1), jnp.stack([came, keep], axis=1)
        )

    grad_final = reduced(dot(grad_logits, w_read, ((1,), (1,)), HALF))
    grad_read = weight_grad(final_in, grad_logits)
    grad_second, gain_final = norm_back(second, gains_full[2], grad_final)
    branch_grad = gathered(grad_second.astype(HALF))
    grad_active = dot(branch_grad, w_down, ((1,), (0,)))
    unused_gelu, gelu_pull = jax.vjp(jax.nn.gelu, hidden_up)
    grad_hidden = gelu_pull(grad_active)[0].astype(HALF)
    grad_mid = reduced(dot(grad_hidden, w_up, ((1,), (1,)), HALF))
    grad_down = weight_grad(branch_grad, active)
    grad_up = weight_grad(normed_mid, grad_hidden)
    grad_mid_in, gain_mid = norm_back(first, gains_full[1], grad_mid)
    grad_first = grad_second + grad_mid_in
    attn_grad = gathered(grad_first.astype(HALF))
    grad_heads = dot(attn_grad, w_out, ((1,), (0,)), HALF).reshape(team, local_heads, HD)
    grad_out_w = weight_grad(attn_grad, flat_heads)
    inner = jnp.einsum("qhd,qhd->hq", grad_heads, attn_heads, preferred_element_type=F32)
    returned = []
    grad_query = jnp.zeros((), F32)
    for back in range(1, per_clip):
        keys_now, values_now = earlier[back - 1]
        more_query, far_keys, far_values = attend_back(
            queries,
            keys_now,
            values_now,
            query_pos,
            query_pos - back * team,
            grad_heads,
            log_total,
            inner,
        )
        grad_query = grad_query + more_query
        returned.append(
            lax.ppermute(
                (far_keys.astype(HALF), far_values.astype(HALF)), "blk", index_of(-back)
            )
        )
    more_query, grad_keys, grad_values = attend_back(
        queries, keys_own, values_own, query_pos, query_pos, grad_heads, log_total, inner
    )
    grad_query = grad_query + more_query
    for far_keys, far_values in returned:
        grad_keys = grad_keys + far_keys.astype(F32)
        grad_values = grad_values + far_values.astype(F32)
    grad_mixed = jnp.concatenate(
        [
            part.astype(HALF).reshape(team, head_columns)
            for part in (grad_query, grad_keys, grad_values)
        ],
        axis=1,
    )
    grad_norm_in = reduced(dot(grad_mixed, w_in, ((1,), (1,)), HALF))
    grad_in = weight_grad(normed_in, grad_mixed)
    grad_embed_in, gain_in = norm_back(embedded_own, gains_full[0], grad_norm_in)
    grad_embed = (grad_first + grad_embed_in).astype(HALF)

    columns_own = lax.all_to_all(grad_embed, "head", 1, 0, tiled=True)

    def token_spread(part, bits):
        pieces = {0: part}
        for bit in bits:
            for mask in list(pieces):
                pieces[mask | bit] = flip(pieces[mask], bit)
        return jnp.concatenate([pieces[mask] for mask in range(blocks)])

    columns_all = jnp.concatenate(
        [
            token_spread(columns_own[:, :mid], bits_a[::-1]),
            token_spread(columns_own[:, mid:], bits_b[::-1]),
        ],
        axis=1,
    )
    grad_table = dot(pick, columns_all, ((0,), (0,)))
    img_sum, code_sum = grad_table[:image_rows], grad_table[image_rows:]

    gain_stack = jnp.stack([gain_in, gain_mid, gain_final])
    gain_parts = jnp.broadcast_to(
        gain_stack.reshape(3, blocks, rows).transpose(1, 0, 2)[:, None],
        (blocks, heads, 3, rows),
    ).reshape(blocks * heads, 3 * rows)
    gain_sum = jnp.sum(lax.all_to_all(gain_parts, both, 0, 0, tiled=True), axis=0).reshape(3, rows)

    in_sum = grad_in.reshape(rows, 2, 3, head_columns).transpose(2, 0, 1, 3).reshape(inward.shape)
    out_sum = grad_out_w.reshape(rows, -1).T
    up_sum = grad_up.reshape(rows, -1)
    down_sum = grad_down.reshape(rows, -1).T
    read_sum = grad_read.reshape(rows, -1)
    sums = [in_sum, out_sum, up_sum, down_sum, img_sum, code_sum, read_sum, gain_sum]
    local_squares = jnp.float32(0.0)
    for shard in sums[:7]:
        local_squares = local_squares + jnp.sum(shard * shard)
    local_squares = local_squares + (head == 0).astype(F32) * jnp.sum(gain_sum * gain_sum)
    mine = jnp.broadcast_to(
        jnp.stack([local_squares, loss_part])[None, :, None], (blocks * heads, 2, 128)
    )
    totals = jnp.sum(lax.all_to_all(mine, both, 0, 0, tiled=True), axis=0)
    grad_norm = jnp.sqrt(totals[0, 0])
    loss_sum = totals[1, 0]
    factor = jnp.minimum(1.0, CLIP / grad_norm)
    spreads = [
        D ** (-0.5),
        (length // 2) ** 0.5 * D ** (-0.5),
        D ** (-0.5),
        FF ** (-0.5),
        0.05,
        0.05,
        2.0 * D ** (-0.5),
    ]
    weights = [inward, outward, expand, contract, image_table, code_table, readout, gains]
    firsts = [
        inward_first,
        outward_first,
        expand_first,
        contract_first,
        image_first,
        code_first,
        readout_first,
        gains_first,
    ]
    seconds = [
        inward_second,
        outward_second,
        expand_second,
        contract_second,
        image_second,
        code_second,
        readout_second,
        gains_second,
    ]
    result = []
    for index in range(8):
        rate = GAIN_RATE if index == 7 else RATE_FACTOR * spreads[index]
        decay = 0.0 if index == 7 else DECAY
        result.extend(
            adamw(weights[index], firsts[index], seconds[index], sums[index] * factor, rate, decay)
        )
    return (*result, loss_sum, loss_count, grad_norm)


def solution(mesh):
    matrices = (
        P(None, "blk", "head"),
        P("head", "blk"),
        P("blk", "head"),
        P("head", "blk"),
        P("blk", "head"),
        P("blk", "head"),
        P("blk", "head"),
        P(None, "blk"),
    )
    tokens = P(None, "blk")
    return jax.shard_map(
        shards,
        mesh=mesh,
        in_specs=matrices * 3 + (tokens, tokens, P(), tokens, tokens),
        out_specs=tuple(spec for spec in matrices for _ in range(3)) + (P(), P(), P()),
        check_vma=False,
    )
```

```python
import jax
import jax.numpy as jnp
from jax import lax
from jax.experimental import pallas as pl
from jax.experimental.layout import Layout, with_layout_constraint
from jax.experimental.pallas import tpu as pltpu
from jax.sharding import PartitionSpec as P

D = 2048
HD = 128
FF = 8192
VT = 1024
VA = 256
STEP = 10


EPS = 1e-05
ZCOEF = 0.01
CLIP = 0.02
BETA1 = 0.9
BETA2 = 0.95
ADAM_EPS = 1e-08
DECAY = 0.1
RATE_FACTOR = 1.5
GAIN_RATE = 0.8

HALF = jnp.bfloat16
F32 = jnp.float32
NEG = -1e30
PAIR = 2


def flip(value, bit):
    count = lax.axis_size("blk")
    return lax.ppermute(value, "blk", [(i, i ^ bit) for i in range(count)])


def rms_norm(hidden, gain):
    return hidden * lax.rsqrt(jnp.mean(hidden * hidden, axis=-1, keepdims=True) + EPS) * gain


def norm_back(hidden, gain, upstream):
    unused, pullback = jax.vjp(rms_norm, hidden, gain)
    return pullback(upstream)


def dot(left, right, dims, out=F32):
    return lax.dot_general(left, right, (dims, ((), ())), preferred_element_type=F32).astype(out)


def adamw(weight, first, second, grad, rate, decay):
    first = BETA1 * first + (1.0 - BETA1) * grad
    second = BETA2 * second + (1.0 - BETA2) * grad * grad
    first_hat = first / (1.0 - BETA1**STEP)
    second_hat = second / (1.0 - BETA2**STEP)
    weight = weight - rate * (first_hat / (jnp.sqrt(second_hat) + ADAM_EPS) + decay * weight)
    return (weight, first, second)


def visible(query_pos, key_pos):
    return (key_pos[None, :] <= query_pos[:, None]) & (key_pos[None, :] >= 0)


def scores_of(queries, keys):
    return HD ** (-0.5) * jnp.einsum("qhd,khd->hqk", queries, keys, preferred_element_type=F32)


def attend(queries, keys, values, query_pos, key_pos, running):
    top_now, total_now, summed = running
    seen = visible(query_pos, key_pos)
    scores = jnp.where(seen, scores_of(queries, keys), NEG)
    top_next = jnp.maximum(top_now, jnp.max(scores, axis=-1))
    weights = jnp.where(seen, jnp.exp(scores - top_next[..., None]), 0.0)
    fading = jnp.exp(top_now - top_next)
    total_next = total_now * fading + jnp.sum(weights, axis=-1)
    summed = summed * fading[..., None] + jnp.einsum(
        "hqk,khd->hqd", weights.astype(HALF), values, preferred_element_type=F32
    )
    return (top_next, total_next, summed)


def attend_back(queries, keys, values, query_pos, key_pos, grad_out, log_total, inner):
    seen = visible(query_pos, key_pos)
    probs = jnp.where(seen, jnp.exp(scores_of(queries, keys) - log_total[..., None]), 0.0)
    grad_values = jnp.einsum(
        "hqk,qhd->khd", probs.astype(HALF), grad_out, preferred_element_type=F32
    )
    grad_probs = jnp.einsum("qhd,khd->hqk", grad_out, values, preferred_element_type=F32)
    grad_scores = (probs * (grad_probs - inner[..., None])).astype(HALF)
    grad_query = HD ** (-0.5) * jnp.einsum(
        "hqk,khd->qhd", grad_scores, keys, preferred_element_type=F32
    )
    grad_keys = HD ** (-0.5) * jnp.einsum(
        "hqk,qhd->khd", grad_scores, queries, preferred_element_type=F32
    )
    return (grad_query, grad_keys, grad_values)


def joined_norm_kernel(blocks_ref, gain_ref, out_ref):
    count, unused, width = blocks_ref.shape
    parts = [blocks_ref[k].astype(F32) for k in range(count)]
    squares = sum(jnp.sum(part * part, axis=-1, keepdims=True) for part in parts)
    scale = lax.rsqrt(squares / (count * width) + EPS)
    for k, part in enumerate(parts):
        at = slice(k * width, (k + 1) * width)
        out_ref[:, at] = (part * scale * gain_ref[:, at]).astype(HALF)


def joined_norm(blocks, gain, count):
    total, tokens, width = blocks.shape
    sides, step = total // count, min(tokens, 128)
    steps = tokens // step
    return pl.pallas_call(
        joined_norm_kernel,
        grid=(sides, steps),
        in_specs=[
            pl.BlockSpec((count, step, width), lambda s, m: (s, m, 0)),
            pl.BlockSpec((1, count * width), lambda s, m: (0, 0)),
        ],
        out_specs=pl.BlockSpec((step, count * width), lambda s, m: (s * steps + m, 0)),
        out_shape=jax.ShapeDtypeStruct((sides * tokens, count * width), HALF),
        cost_estimate=pl.CostEstimate(
            flops=5 * blocks.size, bytes_accessed=4 * blocks.size, transcendentals=0
        ),
    )(blocks, gain[None])


def table_grad_kernel(count, at_ref, *refs):
    pieces, out_ref = refs[:-1], refs[-1]
    split = len(pieces) // count
    tokens, width = pieces[0].shape
    step = out_ref.shape[0]
    row = pl.program_id(0) * step + lax.broadcasted_iota(jnp.int32, (step, tokens), 0)
    for part in range(split):
        total = jnp.zeros((step, width), F32)
        for k in range(count):
            pick = (row == at_ref[k][None, :]).astype(F32).astype(HALF)
            total += jnp.dot(
                pick, pieces[part * count + k][...], preferred_element_type=F32
            )
        out_ref[:, part * width : (part + 1) * width] = total


def table_grad(at, pieces, rows, step):
    count, tokens = at.shape
    width = pieces[0].shape[1]
    columns = width * len(pieces) // count
    return pl.pallas_call(
        lambda *refs: table_grad_kernel(count, *refs),
        grid=(rows // step,),
        in_specs=[pl.BlockSpec((count, tokens), lambda i: (0, 0))]
        + [pl.BlockSpec((tokens, width), lambda i: (0, 0)) for unused in pieces],
        out_specs=pl.BlockSpec((step, columns), lambda i: (i, 0)),
        out_shape=jax.ShapeDtypeStruct((rows, columns), F32),
        compiler_params=pltpu.CompilerParams(vmem_limit_bytes=56 * 2**20),
        cost_estimate=pl.CostEstimate(
            flops=2 * rows * count * tokens * columns,
            bytes_accessed=2 * count * tokens * columns + 4 * rows * columns,
            transcendentals=0,
        ),
    )(at, *pieces)


def assembled_kernel(count, at_ref, *refs):
    pieces, out_ref = refs[:count], refs[count]
    for k, piece in enumerate(pieces):

        @pl.when(pl.program_id(0) == k)
        def write():
            out_ref[0, :, 0] = piece[...]


def assembled_at(places, pieces):
    count = len(pieces)
    unused, rows, columns = pieces[0].shape
    grid = pltpu.PrefetchScalarGridSpec(
        num_scalar_prefetch=1,
        grid=(count,),
        in_specs=[pl.BlockSpec((2, rows, columns), lambda i, at: (0, 0, 0)) for piece in pieces],
        out_specs=pl.BlockSpec(
            (1, 2, 1, rows, columns), lambda i, at: (at[2 * i], 0, at[2 * i + 1], 0, 0)
        ),
    )
    whole = pl.pallas_call(
        lambda *refs: assembled_kernel(count, *refs),
        grid_spec=grid,
        out_shape=jax.ShapeDtypeStruct((count // 2, 2, 2, rows, columns), HALF),
        compiler_params=pltpu.CompilerParams(vmem_limit_bytes=40 * 2**20),
        cost_estimate=pl.CostEstimate(
            flops=0, bytes_accessed=4 * count * pieces[0].size, transcendentals=0
        ),
    )(places, *pieces)
    return whole.reshape(count * 2 * rows, columns)


def shards(
    inward,
    outward,
    expand,
    contract,
    image_table,
    code_table,
    readout,
    gains,
    inward_first,
    outward_first,
    expand_first,
    contract_first,
    image_first,
    code_first,
    readout_first,
    gains_first,
    inward_second,
    outward_second,
    expand_second,
    contract_second,
    image_second,
    code_second,
    readout_second,
    gains_second,
    token_ids,
    modality,
    clip_lengths,
    loss_mask,
    targets,
):
    blocks = lax.axis_size("blk")
    heads = lax.axis_size("head")
    blk = lax.axis_index("blk")
    head = lax.axis_index("head")
    clips, span = token_ids.shape
    length = span * blocks
    rows = D // blocks
    low = blk % 2
    side = (blk // 2) % 2
    high = blk // 4
    highs = blocks // 4
    groups = blocks // 2
    group = high * 2 + low
    per_clip = groups // clips
    clip = group // per_clip
    place = group % per_clip
    ranks = 2 * heads
    rank = side * heads + head
    team = clips * length // groups
    own = team // ranks
    high_bits = [1 << k for k in range(2, blocks.bit_length() - 1)]
    all_bits = [1, 2] + high_bits
    teams = [
        [i * heads + h for i in (base, base + PAIR) for h in range(heads)]
        for base in range(blocks)
        if not base & PAIR
    ]
    both = ("blk", "head")

    def gathered(block):
        return lax.all_gather(block, both, axis=0, tiled=True, axis_index_groups=teams)

    def reduced(partial):
        return lax.psum_scatter(
            partial, both, scatter_dimension=0, tiled=True, axis_index_groups=teams
        ).astype(F32)

    def index_of(shift):
        pairs = []
        for i in range(blocks):
            g = (i // 4) * 2 + i % 2
            far = g + shift
            if 0 <= far < groups and far // per_clip == g // per_clip:
                pairs.append((i, (far // 2) * 4 + (i & PAIR) + far % 2))
        return pairs

    def tie(*values):
        return lax.optimization_barrier(values)

    def sided(weight):
        return weight.astype(HALF).reshape(rows, 2, -1)

    qkv_local = inward.astype(HALF).reshape(3, rows, 2, -1).transpose(1, 2, 0, 3)
    local_first = jnp.concatenate(
        [qkv_local.reshape(rows, 2, -1), sided(outward.astype(HALF).T)], axis=-1
    )
    local = [
        None,
        sided(expand),
        sided(contract.astype(HALF).T),
        sided(readout),
    ]

    small = jnp.concatenate(
        [part.astype(F32).reshape(-1) for part in (token_ids, modality, loss_mask, targets, gains)]
    )[None]
    small = jnp.concatenate([small, flip(small, PAIR)])
    local_first, small = tie(local_first, small)
    masks = [0, PAIR]
    for bit in high_bits + [1]:
        small = jnp.concatenate([small, flip(small, bit)])
        masks = masks + [mask | bit for mask in masks]
    order = blk ^ jnp.arange(blocks)
    small = small[jnp.array([masks.index(mask) for mask in range(blocks)])[order]]
    cells = clips * span
    ids_all, modality_all, mask_all, targets_all = (
        small[:, k * cells : (k + 1) * cells]
        .astype(jnp.int32)
        .reshape(blocks, clips, span)
        .transpose(1, 0, 2)
        .reshape(clips, length)
        for k in range(4)
    )
    gains_full = small[:, 4 * cells :].reshape(blocks, 3, rows).transpose(1, 0, 2).reshape(3, D)

    def paired(halves):
        keep = lax.dynamic_index_in_dim(halves, side, 1, keepdims=False)
        send = lax.dynamic_index_in_dim(halves, 1 - side, 1, keepdims=False)
        came = flip(send, PAIR)
        return jnp.where(side == 0, jnp.stack([keep, came]), jnp.stack([came, keep]))

    def spread_high(mine):
        pieces = [mine]
        for bit in high_bits:
            pieces = pieces + [flip(piece, bit) for piece in pieces]
        return tuple(pieces[1:])

    def spread_low(pieces):
        return tuple(flip(piece, 1) for piece in pieces)

    def assembled(mine, far, near):
        pieces = (mine, *far, *near)
        places = [high ^ (k % highs) if side_at == 0 else low ^ (k // highs)
                  for k in range(len(pieces)) for side_at in range(2)]
        return assembled_at(jnp.stack(places).astype(jnp.int32), pieces)

    mine = [paired(local_first), None, None, None]
    far = [None] * 4
    near = [None] * 4
    mine[1] = paired(local[1])

    def by_device(array):
        split = array.reshape(highs, 2, 2, team // 2)
        return split.transpose(0, 2, 1, 3).reshape(blocks, team // 2)

    image_rows = image_table.shape[0]
    code_local = code_table.shape[0]
    table = jnp.concatenate([image_table.astype(HALF), code_table.astype(HALF)])
    ids_dev, modality_dev = by_device(ids_all)[order], by_device(modality_all)[order]
    code_rows = jnp.clip(jnp.where(modality_dev == 1, ids_dev, VT + ids_dev), 0, VT + VA - 1)
    image_at = ids_dev - blk * image_rows
    code_at = code_rows - blk * code_local
    image_at = jnp.where((image_at >= 0) & (image_at < image_rows), image_at, -1)
    code_at = jnp.where((code_at >= 0) & (code_at < code_local), code_at + image_rows, -1)
    table_at = jnp.where(modality_dev == 0, image_at, code_at)
    table_rows = image_rows + code_local
    pick = (table_at.reshape(-1)[:, None] == jnp.arange(table_rows)[None, :]).astype(HALF)
    picked = dot(pick, table, ((1,), (0,)), HALF)
    width = table.shape[1]
    levels = len(all_bits)
    picked = picked.reshape((2,) * levels + (team // 2, width))

    def token_hop(part, bit, left):
        axis = left.index(bit)
        keep = lax.index_in_dim(part, 0, axis, keepdims=False)
        send = lax.index_in_dim(part, 1, axis, keepdims=False)
        return keep + flip(send, bit)

    left = sorted(all_bits, reverse=True)
    mid = width // 2
    picked, mine[0] = tie(picked, mine[0])
    far[0] = spread_high(mine[0])
    part_a = token_hop(picked[..., :mid], 1, left)
    part_b = token_hop(picked[..., mid:], PAIR, left)
    part_a = token_hop(part_a, PAIR, left[:-1])
    part_b = token_hop(part_b, 1, left[:-2] + left[-1:])
    part_a, part_b, mine[0], mine[1], *far[0] = tie(part_a, part_b, mine[0], mine[1], *far[0])
    near_own = spread_low(mine[:1])
    for k, bit in enumerate(high_bits[::-1]):
        part_a = token_hop(part_a, bit, left[k:-2])
        part_b = token_hop(part_b, bit, left[k:-2])
    block = jnp.concatenate([part_a, part_b], axis=-1)
    block, mine[1], *near_own = tie(block, mine[1], *near_own)
    far[1] = spread_high(mine[1])
    near[0] = (*near_own, *spread_low(tie(*far[0], block)[:-1]))
    near_own = spread_low(tie(mine[1], block)[:1])
    columns_in = gathered(block).reshape(ranks, team // 2, width)
    normed_in = joined_norm(columns_in, gains_full[0], heads)
    embedded_own = (
        lax.dynamic_slice(columns_in, (side * heads, head * own, 0), (heads, own, width))
        .transpose(1, 0, 2)
        .reshape(own, heads * width)
        .astype(F32)
    )
    w_first = assembled(mine[0], far[0], near[0])
    head_columns = w_first.shape[-1] // 4
    w_in, w_out = w_first[:, : 3 * head_columns], w_first[:, 3 * head_columns :]
    local_heads = head_columns // HD
    mixed = dot(normed_in, w_in, ((1,), (0,)), HALF)
    mixed, mine[1], local[2], local[3], near_own, *far[1] = tie(
        mixed, mine[1], local[2], local[3], *near_own, *far[1]
    )
    mine[2], mine[3] = paired(local[2]), paired(local[3])
    queries, keys_own, values_own = (
        mixed[:, k * head_columns : (k + 1) * head_columns].reshape(team, local_heads, HD)
        for k in range(3)
    )
    offsets = jnp.arange(team)
    query_pos = place * team + offsets
    running = (
        jnp.full((local_heads, team), NEG, F32),
        jnp.zeros((local_heads, team), F32),
        jnp.zeros((local_heads, team, HD), F32),
    )
    earlier = []
    for back in range(1, per_clip):
        earlier.append(lax.ppermute((keys_own, values_own), "blk", index_of(back)))
    running = attend(queries, keys_own, values_own, query_pos, query_pos, running)
    *far[1], mine[2], earlier = tie(*far[1], mine[2], earlier)
    near[1] = (near_own, *spread_low(far[1]))
    far[2] = spread_high(mine[2])
    near_own = spread_low(mine[2:3])
    for back in range(1, per_clip):
        keys_now, values_now = earlier[back - 1]
        running = attend(
            queries, keys_now, values_now, query_pos, query_pos - back * team, running
        )
    top_all, total_all, summed = running
    log_total = top_all + jnp.log(total_all)
    attn_heads = (summed / total_all[..., None]).transpose(1, 0, 2).astype(HALF)
    flat_heads = attn_heads.reshape(team, head_columns)
    flat_heads, mine[3] = tie(flat_heads, mine[3])
    first = embedded_own + reduced(dot(flat_heads, w_out, ((1,), (1,)), HALF))
    w_up = assembled(mine[1], far[1], near[1])
    first, w_up, mine[3], near_own, *far[2] = tie(first, w_up, mine[3], *near_own, *far[2])
    far[3] = spread_high(mine[3])
    near[2] = (near_own, *spread_low(far[2]))
    normed_mid, *near_2 = tie(gathered(rms_norm(first, gains_full[1]).astype(HALF)), *near[2])
    w_down = assembled(mine[2], far[2], near_2)
    hidden_up = dot(normed_mid, w_up, ((1,), (0,)))
    active = jax.nn.gelu(hidden_up).astype(HALF)
    active, mine[3], *far[3] = tie(active, mine[3], *far[3])
    near[3] = spread_low((mine[3], *far[3]))
    second = first + reduced(dot(active, w_down, ((1,), (1,)), HALF))
    second, *near_3 = tie(second, *near[3])
    w_read = assembled(mine[3], far[3], near_3)
    final_in, w_read = tie(gathered(rms_norm(second, gains_full[2]).astype(HALF)), w_read)
    logits = dot(final_in, w_read, ((1,), (0,)))

    def of_team(array):
        return lax.dynamic_slice(array, (clip, place * team), (1, team))[0]

    weight_all = (
        (mask_all == 1) & (jnp.arange(length)[None, :] < clip_lengths[:, None])
    ).astype(F32)
    loss_count = jnp.sum(weight_all)
    weight_of = of_team(weight_all)
    targets_own = of_team(targets_all)
    vocab_local = logits.shape[1]
    column_ids = (head * 2 + side) * vocab_local + jnp.arange(vocab_local)
    match = column_ids[None, :] == targets_own[:, None]
    top_vocab = jnp.max(logits, axis=-1)
    sum_vocab = jnp.sum(jnp.exp(logits - top_vocab[:, None]), axis=-1)
    hit_vocab = jnp.sum(jnp.where(match, logits, 0.0), axis=-1)
    stats = jnp.stack([top_vocab, sum_vocab, hit_vocab])
    steps = [("blk", PAIR)] + [("head", 1 << k) for k in range(heads.bit_length() - 1)]
    for axis, bit in steps:
        pairs = [(i, i ^ bit) for i in range(lax.axis_size(axis))]
        other = lax.ppermute(stats, axis, pairs)
        top = jnp.maximum(stats[0], other[0])
        total = stats[1] * jnp.exp(stats[0] - top) + other[1] * jnp.exp(other[0] - top)
        stats = jnp.stack([top, total, stats[2] + other[2]])
    log_norm = stats[0] + jnp.log(stats[1])
    per_token = (log_norm + ZCOEF * log_norm * log_norm - stats[2]) * weight_of
    loss_part = jnp.sum(per_token) * (rank == 0).astype(F32)

    token_grad = weight_of / loss_count
    probs = jnp.exp(logits - log_norm[:, None])
    grad_logits = (
        token_grad[:, None]
        * (probs * (1.0 + 2.0 * ZCOEF * log_norm)[:, None] - match.astype(F32))
    ).astype(HALF)

    top_bit = high_bits[-1]
    top = (blk // top_bit) % 2

    def made_of(left, right):
        return dot(left, right, ((0,), (0,)), HALF).reshape(
            2, highs // 2, 2, 2, rows, right.shape[1]
        )

    def low_part(made, at_top, at_low):
        chosen = lax.dynamic_index_in_dim(made, at_top, 0, keepdims=False)
        return lax.dynamic_index_in_dim(chosen, at_low, 2, keepdims=False)

    def send_low(made, at_top):
        return flip(low_part(made, at_top, 1 - low), 1)

    def add_low(made, at_top, came):
        return low_part(made, at_top, low).astype(F32) + came.astype(F32)

    def send_high(made, came):
        return flip(add_low(made, 1 - top, came).astype(HALF), top_bit)

    def add_high(made, came_low, came_high):
        total = add_low(made, top, came_low) + came_high.astype(F32)
        total = total.reshape((2,) * (len(high_bits) - 1) + total.shape[1:])
        for bit in high_bits[-2::-1] if len(high_bits) > 1 else []:
            at = (blk // bit) % 2
            send = lax.dynamic_index_in_dim(total, 1 - at, 0, keepdims=False)
            keep = lax.dynamic_index_in_dim(total, at, 0, keepdims=False)
            total = keep + flip(send.astype(HALF), bit).astype(F32)
        return total

    def sum_sides(total):
        send = lax.dynamic_index_in_dim(total, 1 - side, 0, keepdims=False)
        keep = lax.dynamic_index_in_dim(total, side, 0, keepdims=False)
        came = flip(send.astype(HALF), PAIR).astype(F32)
        return jnp.where(side == 0, keep, came), jnp.where(side == 0, came, keep)

    grad_final = reduced(dot(grad_logits, w_read, ((1,), (1,)), HALF))
    read_made = made_of(final_in, grad_logits)
    read_far = send_low(read_made, 1 - top)
    grad_final, read_made, read_far = tie(grad_final, read_made, read_far)
    read_near = send_low(read_made, top)
    read_high = send_high(read_made, read_far)
    grad_second, gain_final = norm_back(second, gains_full[2], grad_final)
    branch_grad = gathered(grad_second.astype(HALF))
    branch_grad, read_near = tie(branch_grad, read_near)
    grad_active = dot(branch_grad, w_down, ((1,), (0,)))
    unused_gelu, gelu_pull = jax.vjp(jax.nn.gelu, hidden_up)
    grad_hidden = gelu_pull(grad_active)[0].astype(HALF)
    grad_hidden, read_high = tie(grad_hidden, read_high)
    grad_mid = reduced(dot(grad_hidden, w_up, ((1,), (1,)), HALF))
    read_total = add_high(read_made, read_near, read_high)
    down_made = made_of(branch_grad, active)
    down_far = send_low(down_made, 1 - top)
    grad_mid, read_total, down_made, down_far = tie(grad_mid, read_total, down_made, down_far)
    down_near = send_low(down_made, top)
    down_high = send_high(down_made, down_far)
    grad_mid_in, gain_mid = norm_back(first, gains_full[1], grad_mid)
    grad_first = grad_second + grad_mid_in
    attn_grad = gathered(grad_first.astype(HALF))
    up_made = made_of(normed_mid, grad_hidden)
    attn_grad, up_made, down_near = tie(attn_grad, up_made, down_near)
    up_far = send_low(up_made, 1 - top)
    grad_read = sum_sides(read_total)
    grad_heads = dot(attn_grad, w_out, ((1,), (0,)), HALF).reshape(team, local_heads, HD)
    inner = jnp.einsum("qhd,qhd->hq", grad_heads, attn_heads, preferred_element_type=F32)
    returned = []
    grad_query = jnp.zeros((), F32)
    grad_down = sum_sides(add_high(down_made, down_near, down_high))
    for back in range(1, per_clip):
        keys_now, values_now = earlier[back - 1]
        more_query, far_keys, far_values = attend_back(
            queries,
            keys_now,
            values_now,
            query_pos,
            query_pos - back * team,
            grad_heads,
            log_total,
            inner,
        )
        grad_query = grad_query + more_query
        returned.append(
            lax.ppermute(
                (far_keys.astype(HALF), far_values.astype(HALF)), "blk", index_of(-back)
            )
        )
    more_query, grad_keys, grad_values = attend_back(
        queries, keys_own, values_own, query_pos, query_pos, grad_heads, log_total, inner
    )
    grad_query = grad_query + more_query
    for far_keys, far_values in returned:
        grad_keys = grad_keys + far_keys.astype(F32)
        grad_values = grad_values + far_values.astype(F32)
    grad_mixed = jnp.concatenate(
        [
            part.astype(HALF).reshape(team, head_columns)
            for part in (grad_query, grad_keys, grad_values)
        ],
        axis=1,
    )
    grad_mixed, up_made, up_far, grad_down, grad_read = tie(
        grad_mixed, up_made, up_far, grad_down, grad_read
    )
    up_near = send_low(up_made, top)
    up_high = send_high(up_made, up_far)
    grad_norm_in = reduced(dot(grad_mixed, w_in, ((1,), (1,)), HALF))
    in_made = made_of(normed_in, grad_mixed)
    out_made = made_of(attn_grad, flat_heads)
    in_far, out_far = send_low(in_made, 1 - top), send_low(out_made, 1 - top)
    grad_norm_in, up_near, up_high, in_made, out_made, in_far, out_far = tie(
        grad_norm_in, up_near, up_high, in_made, out_made, in_far, out_far
    )
    grad_up = sum_sides(add_high(up_made, up_near, up_high))
    grad_embed_in, gain_in = norm_back(embedded_own, gains_full[0], grad_norm_in)
    grad_embed = (grad_first + grad_embed_in).astype(HALF)

    columns_own = lax.all_to_all(grad_embed, "head", 1, 0, tiled=True)

    gain_sum = jnp.stack([gain_in, gain_mid, gain_final]).reshape(
        (3,) + (2,) * len(all_bits) + (rows,)
    )

    def gain_hop(total, bit, left):
        axis = 1 + left.index(bit)
        at = (blk // bit) % 2
        send = lax.dynamic_index_in_dim(total, 1 - at, axis, keepdims=False)
        keep = lax.dynamic_index_in_dim(total, at, axis, keepdims=False)
        return keep + flip(send, bit)

    def spread(pieces, bit):
        return pieces + [flip(piece, bit) for piece in pieces]

    pieces_a, pieces_b = [columns_own[:, :mid]], [columns_own[:, mid:]]
    in_near, out_near = send_low(in_made, top), send_low(out_made, top)
    for k, bit in enumerate(high_bits[::-1]):
        pieces_a, pieces_b = spread(pieces_a, bit), spread(pieces_b, bit)
        gain_sum = gain_hop(gain_sum, bit, left[k:])
    pieces_a, pieces_b, gain_sum, in_far, out_far, in_near, out_near, grad_up = tie(
        pieces_a, pieces_b, gain_sum, in_far, out_far, in_near, out_near, grad_up
    )
    in_high, out_high = send_high(in_made, in_far), send_high(out_made, out_far)
    pieces_a, pieces_b = spread(pieces_a, PAIR), spread(pieces_b, 1)
    gain_sum = gain_hop(gain_sum, 1, left[-2:])
    pieces_a, pieces_b, gain_sum = tie(pieces_a, pieces_b, gain_sum)
    pieces_a, pieces_b = spread(pieces_a, 1), spread(pieces_b, PAIR)
    gain_sum = gain_hop(gain_sum, PAIR, left[-2:-1])
    pieces_a, pieces_b, gain_sum, in_high, out_high = tie(
        pieces_a, pieces_b, gain_sum, in_high, out_high
    )
    grad_in = sum_sides(add_high(in_made, in_near, in_high))
    grad_out_w = sum_sides(add_high(out_made, out_near, out_high))
    for k in range(heads.bit_length() - 1):
        pairs = [(i, i ^ (1 << k)) for i in range(heads)]
        gain_sum = gain_sum + lax.ppermute(gain_sum, "head", pairs)
    masks_a, masks_b = [0], [0]
    for bit_a, bit_b in zip(high_bits[::-1] + [PAIR, 1], high_bits[::-1] + [1, PAIR]):
        masks_a = masks_a + [mask | bit_a for mask in masks_a]
        masks_b = masks_b + [mask | bit_b for mask in masks_b]
    token_pieces = [pieces_a[masks_a.index(mask)] for mask in range(blocks)] + [
        pieces_b[masks_b.index(mask)] for mask in range(blocks)
    ]
    row_step = max(s for s in range(8, 321, 8) if table_rows % s == 0)
    grad_table = table_grad(table_at, token_pieces, table_rows, row_step)
    img_sum, code_sum = grad_table[:image_rows], grad_table[image_rows:]

    in_sum = jnp.stack(
        [
            jnp.concatenate(
                [part[:, k * head_columns : (k + 1) * head_columns] for part in grad_in], axis=1
            )
            for k in range(3)
        ]
    )
    out_sum = jnp.concatenate([part.T for part in grad_out_w])
    down_sum = jnp.concatenate([part.T for part in grad_down])
    up_sum = jnp.concatenate(grad_up, axis=1)
    read_sum = jnp.concatenate(grad_read, axis=1)
    in_sum, out_sum, up_sum, down_sum, read_sum = (
        with_layout_constraint(total, Layout(major_to_minor=tuple(range(total.ndim))))
        for total in (in_sum, out_sum, up_sum, down_sum, read_sum)
    )
    sums = [in_sum, out_sum, up_sum, down_sum, img_sum, code_sum, read_sum, gain_sum]
    local_squares = jnp.float32(0.0)
    for shard in sums[:7]:
        local_squares = local_squares + jnp.sum(shard * shard)
    local_squares = local_squares + (head == 0).astype(F32) * jnp.sum(gain_sum * gain_sum)
    mine = jnp.broadcast_to(
        jnp.stack([local_squares, loss_part])[None, :, None], (blocks * heads, 2, 128)
    )
    totals = jnp.sum(lax.all_to_all(mine, both, 0, 0, tiled=True), axis=0)
    grad_norm = jnp.sqrt(totals[0, 0])
    loss_sum = totals[1, 0]
    factor = jnp.minimum(1.0, CLIP / grad_norm)
    spreads = [
        D ** (-0.5),
        (length // 2) ** 0.5 * D ** (-0.5),
        D ** (-0.5),
        FF ** (-0.5),
        0.05,
        0.05,
        2.0 * D ** (-0.5),
    ]
    weights = [inward, outward, expand, contract, image_table, code_table, readout, gains]
    firsts = [
        inward_first,
        outward_first,
        expand_first,
        contract_first,
        image_first,
        code_first,
        readout_first,
        gains_first,
    ]
    seconds = [
        inward_second,
        outward_second,
        expand_second,
        contract_second,
        image_second,
        code_second,
        readout_second,
        gains_second,
    ]
    result = []
    for index in range(8):
        rate = GAIN_RATE if index == 7 else RATE_FACTOR * spreads[index]
        decay = 0.0 if index == 7 else DECAY
        result.extend(
            adamw(weights[index], firsts[index], seconds[index], sums[index] * factor, rate, decay)
        )
    return (*result, loss_sum, loss_count, grad_norm)


def solution(mesh):
    matrices = (
        P(None, "blk", "head"),
        P("head", "blk"),
        P("blk", "head"),
        P("head", "blk"),
        P("blk", "head"),
        P("blk", "head"),
        P("blk", "head"),
        P(None, "blk"),
    )
    tokens = P(None, "blk")
    return jax.shard_map(
        shards,
        mesh=mesh,
        in_specs=matrices * 3 + (tokens, tokens, P(), tokens, tokens),
        out_specs=tuple(spec for spec in matrices for _ in range(3)) + (P(), P(), P()),
        check_vma=False,
    )
```

```python
import jax
import jax.numpy as jnp
import numpy as np
from jax import lax
from jax.experimental import pallas as pl
from jax.experimental.layout import Layout, with_layout_constraint
from jax.experimental.pallas import tpu as pltpu
from jax.sharding import PartitionSpec as P

D = 2048
HD = 128
FF = 8192
VT = 1024
VA = 256
STEP = 10


EPS = 1e-05
ZCOEF = 0.01
CLIP = 0.02
BETA1 = 0.9
BETA2 = 0.95
ADAM_EPS = 1e-08
DECAY = 0.1
RATE_FACTOR = 1.5
GAIN_RATE = 0.8

HALF = jnp.bfloat16
F32 = jnp.float32
NEG = -1e30
LOG2E = 1.4426950408889634
SCORE = HD ** (-0.5) * LOG2E
PAIR = 2


def flip(value, bit):
    count = lax.axis_size("blk")
    return lax.ppermute(value, "blk", [(i, i ^ bit) for i in range(count)])


def rms_norm(hidden, gain):
    return hidden * lax.rsqrt(jnp.mean(hidden * hidden, axis=-1, keepdims=True) + EPS) * gain


def norm_back(hidden, gain, upstream):
    unused, pullback = jax.vjp(rms_norm, hidden, gain)
    return pullback(upstream)


def dot(left, right, dims, out=F32):
    return lax.dot_general(left, right, (dims, ((), ())), preferred_element_type=F32).astype(out)


def adamw(weight, first, second, grad, rate, decay):
    first = BETA1 * first + (1.0 - BETA1) * grad
    second = BETA2 * second + (1.0 - BETA2) * grad * grad
    first_hat = first / (1.0 - BETA1**STEP)
    second_hat = second / (1.0 - BETA2**STEP)
    weight = weight - rate * (first_hat / (jnp.sqrt(second_hat) + ADAM_EPS) + decay * weight)
    return (weight, first, second)


def dot_last(left, right):
    return lax.dot_general(left, right, (((1,), (1,)), ((), ())), preferred_element_type=F32)


def dot_first(left, right):
    return lax.dot_general(left, right, (((0,), (0,)), ((), ())), preferred_element_type=F32)


def attend_kernel(opening, closing, qpos_ref, kpos_ref, q_ref, k_ref, v_ref, *refs):
    scores = dot_last(k_ref[...], q_ref[...]) * SCORE
    scores = jnp.where(kpos_ref[...] <= qpos_ref[...], scores, NEG)
    top = jnp.max(scores, axis=0, keepdims=True)
    if not opening:
        acc_in, top_in, total_in = refs[:3]
        refs = refs[3:]
        top = jnp.maximum(top, top_in[0])
    weights = jnp.exp2(scores - top)
    total = jnp.sum(weights, axis=0, keepdims=True)
    acc = dot_first(v_ref[...], weights.astype(HALF))
    if not opening:
        fading = jnp.exp2(top_in[0] - top)
        total = total + total_in[0] * fading
        acc = acc + acc_in[0] * fading
    if closing:
        out_ref, log_ref = refs
        out_ref[...] = (acc / total).T.astype(HALF)
        log_ref[0] = top + jnp.log2(total)
    else:
        acc_ref, top_ref, total_ref = refs
        acc_ref[0] = acc
        top_ref[0] = top
        total_ref[0] = total


def attend(queries, pairs, at, query_pos, key_pos, state, closing, count):
    team = queries.shape[0]
    step = min(team, 256)
    row = pl.BlockSpec((1, 1, step), lambda h, i: (h, 0, i))
    wide = pl.BlockSpec((1, HD, step), lambda h, i: (h, 0, i))
    rows = jax.ShapeDtypeStruct((count, 1, team), F32)
    if closing:
        out_specs = [pl.BlockSpec((step, HD), lambda h, i: (i, h)), row]
        out_shape = [jax.ShapeDtypeStruct((team, count * HD), HALF), rows]
    else:
        out_specs = [wide, row, row]
        out_shape = [jax.ShapeDtypeStruct((count, HD, team), F32), rows, rows]
    return pl.pallas_call(
        lambda *refs: attend_kernel(not state, closing, *refs),
        grid=(count, team // step),
        in_specs=[
            pl.BlockSpec((1, step), lambda h, i: (0, i)),
            pl.BlockSpec((team, 1), lambda h, i: (0, 0)),
            pl.BlockSpec((step, HD), lambda h, i: (i, h)),
            pl.BlockSpec((team, HD), lambda h, i: (0, at + h)),
            pl.BlockSpec((team, HD), lambda h, i: (0, at + count + h)),
        ]
        + ([wide, row, row] if state else []),
        out_specs=out_specs,
        out_shape=out_shape,
        compiler_params=pltpu.CompilerParams(vmem_limit_bytes=40 * 2**20),
        cost_estimate=pl.CostEstimate(
            flops=4 * count * team * team * HD,
            bytes_accessed=10 * count * team * HD,
            transcendentals=count * team * team,
        ),
    )(query_pos[None], key_pos[:, None], queries, pairs, pairs, *state)


def attend_back_kernel(opening, closing, qpos_ref, kpos_ref, q_ref, k_ref, v_ref, *refs):
    out_ref, grad_ref, log_ref = refs[:3]
    query_in, (query_ref, pair_ref, keys_acc, values_acc) = refs[3:-4], refs[-4:]
    head, step = pl.program_id(0), pl.program_id(1)
    grad = grad_ref[...]
    inner = (grad.astype(F32) * out_ref[...].astype(F32)).T
    inner = jnp.sum(inner, axis=0, keepdims=True)
    scores = dot_last(k_ref[...], q_ref[...]) * SCORE
    seen = kpos_ref[...] <= qpos_ref[...]
    probs = jnp.where(seen, jnp.exp2(scores - log_ref[0]), 0.0)
    grad_probs = dot_last(v_ref[...], grad)
    grad_scores = (probs * (grad_probs - inner)).astype(HALF)
    grad_query = dot_first(k_ref[...], grad_scores)
    if not opening:
        grad_query = grad_query + query_in[0][0]
    if closing:
        query_ref[...] = (grad_query * HD ** (-0.5)).T.astype(HALF)
    else:
        query_ref[0] = grad_query

    @pl.when(step == 0)
    def clear():
        keys_acc[...] = jnp.zeros_like(keys_acc)
        values_acc[...] = jnp.zeros_like(values_acc)

    keys_acc[...] += jnp.dot(grad_scores, q_ref[...], preferred_element_type=F32)
    values_acc[...] += jnp.dot(probs.astype(HALF), grad, preferred_element_type=F32)

    @pl.when(step == pl.num_programs(1) - 1)
    def write():
        half = pair_ref.shape[1] // 2
        at = pl.multiple_of(head * HD, HD)
        pair_ref[:, pl.ds(at, HD)] = (keys_acc[...] * HD ** (-0.5)).astype(pair_ref.dtype)
        pair_ref[:, pl.ds(half + at, HD)] = values_acc[...].astype(pair_ref.dtype)


def attend_back(queries, pairs, at, query_pos, key_pos, out, grad, log_total, state, closing, count):
    team = queries.shape[0]
    step = min(team, 256)
    wide = pl.BlockSpec((1, HD, step), lambda h, i: (h, 0, i))
    block = pl.BlockSpec((step, HD), lambda h, i: (i, h))
    if closing:
        query_spec, query_shape = block, jax.ShapeDtypeStruct((team, count * HD), HALF)
    else:
        query_spec, query_shape = wide, jax.ShapeDtypeStruct((count, HD, team), F32)
    return pl.pallas_call(
        lambda *refs: attend_back_kernel(state is None, closing, *refs),
        grid=(count, team // step),
        in_specs=[
            pl.BlockSpec((1, step), lambda h, i: (0, i)),
            pl.BlockSpec((team, 1), lambda h, i: (0, 0)),
            block,
            pl.BlockSpec((team, HD), lambda h, i: (0, at + h)),
            pl.BlockSpec((team, HD), lambda h, i: (0, at + count + h)),
            block,
            block,
            pl.BlockSpec((1, 1, step), lambda h, i: (h, 0, i)),
        ]
        + ([] if state is None else [wide]),
        out_specs=[query_spec, pl.BlockSpec((team, 2 * count * HD), lambda h, i: (0, 0))],
        out_shape=[
            query_shape,
            jax.ShapeDtypeStruct((team, 2 * count * HD), F32 if closing else HALF),
        ],
        scratch_shapes=[pltpu.VMEM((team, HD), F32), pltpu.VMEM((team, HD), F32)],
        compiler_params=pltpu.CompilerParams(vmem_limit_bytes=48 * 2**20),
        cost_estimate=pl.CostEstimate(
            flops=10 * count * team * team * HD,
            bytes_accessed=20 * count * team * HD,
            transcendentals=count * team * team,
        ),
    )(
        query_pos[None],
        key_pos[:, None],
        queries,
        pairs,
        pairs,
        out,
        grad,
        log_total,
        *([] if state is None else [state]),
    )


def joined_norm_kernel(sides, at_ref, gain_ref, *refs):
    pieces, out_ref, first_ref = refs[:-2], refs[-2], refs[-1]
    count = len(pieces) // sides
    width = pieces[0].shape[1]
    is_first = (pl.program_id(0) == 0) & (pl.program_id(1) == 0)
    for side in range(sides):
        parts = [ref[...].astype(F32) for ref in pieces[side * count : (side + 1) * count]]
        squares = sum(jnp.sum(part * part, axis=-1, keepdims=True) for part in parts)
        scale = lax.rsqrt(squares / (count * width) + EPS)
        for k, part in enumerate(parts):
            at = pl.ds(pl.multiple_of(at_ref[k] * width, width), width)
            out_ref[0, side, 0, :, at] = (part * scale * gain_ref[:, at]).astype(HALF)
            if side == 0:

                @pl.when(is_first)
                def keep():
                    first_ref[:, at] = part


def joined_norm(pieces, at, gain, own):
    ys = len(pieces[0][0])
    width = pieces[0][0][0].shape[1]
    columns = 2 * ys * width
    flat, specs = [], []
    for of_side in pieces:
        for core, of_core in enumerate(of_side):
            for y, piece in enumerate(of_core):
                flat.append(piece)
                specs.append(
                    pl.BlockSpec(
                        (own, width),
                        lambda c, k, at, core=core, y=y: ((c ^ core) * ys + (k ^ y), 0),
                    )
                )
    grid = pltpu.PrefetchScalarGridSpec(
        num_scalar_prefetch=1,
        grid=(2, ys),
        in_specs=[pl.BlockSpec((1, columns), lambda c, k, at: (0, 0))] + specs,
        out_specs=[
            pl.BlockSpec((1, 2, 1, own, columns), lambda c, k, at: (c, 0, k, 0, 0)),
            pl.BlockSpec((own, columns), lambda c, k, at: (0, 0)),
        ],
    )
    normed, first = pl.pallas_call(
        lambda *refs: joined_norm_kernel(2, *refs),
        grid_spec=grid,
        out_shape=[
            jax.ShapeDtypeStruct((2, 2, ys, own, columns), HALF),
            jax.ShapeDtypeStruct((own, columns), F32),
        ],
        compiler_params=pltpu.CompilerParams(vmem_limit_bytes=60 * 2**20),
        cost_estimate=pl.CostEstimate(
            flops=20 * ys * own * columns, bytes_accessed=16 * ys * own * columns, transcendentals=0
        ),
    )(at, gain[None], *flat)
    return normed.reshape(4 * ys * own, columns), first


def table_grad_kernel(places, at_ref, *refs):
    parts, out_ref = refs[:-1], refs[-1]
    tokens = at_ref.shape[1]
    width = parts[0].shape[2]
    step = out_ref.shape[0]
    row = pl.program_id(0) * step + lax.broadcasted_iota(jnp.int32, (step, tokens), 0)
    for part, order in enumerate(places):
        total = jnp.zeros((step, width), F32)
        for k, place in enumerate(order):
            pieces, at = parts[2 * part + place // (len(order) // 2)], place % (len(order) // 2)
            pick = (row == at_ref[k][None, :]).astype(F32).astype(HALF)
            total += jnp.dot(pick, pieces[at, :tokens], preferred_element_type=F32)
        out_ref[:, part * width : (part + 1) * width] = total


def table_grad(at, parts, places, rows, step):
    count, tokens = at.shape
    columns = parts[0].shape[2] * len(places)
    return pl.pallas_call(
        lambda *refs: table_grad_kernel(places, *refs),
        grid=(rows // step,),
        in_specs=[pl.BlockSpec((count, tokens), lambda i: (0, 0))]
        + [pl.BlockSpec(part.shape, lambda i: (0, 0, 0)) for part in parts],
        out_specs=pl.BlockSpec((step, columns), lambda i: (i, 0)),
        out_shape=jax.ShapeDtypeStruct((rows, columns), F32),
        compiler_params=pltpu.CompilerParams(vmem_limit_bytes=56 * 2**20),
        cost_estimate=pl.CostEstimate(
            flops=2 * rows * count * tokens * columns,
            bytes_accessed=2 * count * tokens * columns + 4 * rows * columns,
            transcendentals=0,
        ),
    )(at, *parts)


def assembled_kernel(count, at_ref, *refs):
    pieces, out_ref = refs[:count], refs[count]
    for k, piece in enumerate(pieces):

        @pl.when(pl.program_id(0) == k)
        def write():
            out_ref[0, :, 0] = piece[...]


def assembled_at(places, pieces):
    count = len(pieces)
    unused, rows, columns = pieces[0].shape
    grid = pltpu.PrefetchScalarGridSpec(
        num_scalar_prefetch=1,
        grid=(count,),
        in_specs=[pl.BlockSpec((2, rows, columns), lambda i, at: (0, 0, 0)) for piece in pieces],
        out_specs=pl.BlockSpec(
            (1, 2, 1, rows, columns), lambda i, at: (at[2 * i], 0, at[2 * i + 1], 0, 0)
        ),
    )
    whole = pl.pallas_call(
        lambda *refs: assembled_kernel(count, *refs),
        grid_spec=grid,
        out_shape=jax.ShapeDtypeStruct((count // 2, 2, 2, rows, columns), HALF),
        compiler_params=pltpu.CompilerParams(vmem_limit_bytes=60 * 2**20),
        cost_estimate=pl.CostEstimate(
            flops=0, bytes_accessed=4 * count * pieces[0].size, transcendentals=0
        ),
    )(places, *pieces)
    return whole.reshape(count * 2 * rows, columns)


def shards(
    inward,
    outward,
    expand,
    contract,
    image_table,
    code_table,
    readout,
    gains,
    inward_first,
    outward_first,
    expand_first,
    contract_first,
    image_first,
    code_first,
    readout_first,
    gains_first,
    inward_second,
    outward_second,
    expand_second,
    contract_second,
    image_second,
    code_second,
    readout_second,
    gains_second,
    token_ids,
    modality,
    clip_lengths,
    loss_mask,
    targets,
):
    blocks = lax.axis_size("blk")
    heads = lax.axis_size("head")
    blk = lax.axis_index("blk")
    head = lax.axis_index("head")
    clips, span = token_ids.shape
    length = span * blocks
    rows = D // blocks
    low = blk % 2
    side = (blk // 2) % 2
    high = blk // 4
    highs = blocks // 4
    groups = blocks // 2
    group = high * 2 + low
    per_clip = groups // clips
    clip = group // per_clip
    place = group % per_clip
    ranks = 2 * heads
    core, y_at, ys = head % 2, head // 2, heads // 2
    rank = side * heads + head
    team = clips * length // groups
    half = team // 2
    own = team // ranks
    high_bits = [1 << k for k in range(2, blocks.bit_length() - 1)]
    all_bits = [1, 2] + high_bits
    both = ("blk", "head")
    near_peers = [(side_bit, 2 * y) for side_bit in (0, PAIR) for y in range(ys)][1:]

    def hop(value, blk_bits, head_bits):
        pairs = [
            (i * heads + h, (i ^ blk_bits) * heads + (h ^ head_bits))
            for i in range(blocks)
            for h in range(heads)
        ]
        return lax.ppermute(value, both, pairs)

    def tie(*values):
        return lax.optimization_barrier(values)

    def gathered(block, *riders):
        parts, riders = tie([hop(block, *bits) for bits in near_peers], riders)
        mine = jnp.concatenate([block] + parts)
        return ((mine, hop(mine, 0, 1)), *riders)

    def core_sum(mine, other, weight, dims):
        came = hop(dot(other, weight, dims, HALF), 0, 1)
        (made,) = tie(dot(mine, weight, dims, HALF))
        made = (made.astype(F32) + came.astype(F32)).astype(HALF)
        return made.reshape(ranks // 2, own, D)

    def group_sum(made, *riders):
        parts = [hop(made[k + 1], *bits) for k, bits in enumerate(near_peers)]
        parts, riders = tie(parts, riders)
        return (sum((part.astype(F32) for part in parts), made[0].astype(F32)), *riders)

    def index_of(shift):
        pairs = []
        for i in range(blocks):
            g = (i // 4) * 2 + i % 2
            far = g + shift
            if 0 <= far < groups and far // per_clip == g // per_clip:
                pairs.append((i, (far // 2) * 4 + (i & PAIR) + far % 2))
        return pairs

    def sided(weight):
        return weight.astype(HALF).reshape(rows, 2, -1)

    qkv_local = inward.astype(HALF).reshape(3, rows, 2, -1).transpose(1, 2, 0, 3)
    local_first = jnp.concatenate(
        [qkv_local.reshape(rows, 2, -1), sided(outward.astype(HALF).T)], axis=-1
    )
    local = [
        None,
        sided(expand),
        sided(contract.astype(HALF).T),
        sided(readout),
    ]

    def sides_of(halves):
        return tuple(
            lax.dynamic_index_in_dim(halves, at, 1, keepdims=False) for at in (side, 1 - side)
        )

    def paired(keep, send):
        came = flip(send, PAIR)
        return jnp.where(side == 0, jnp.stack([keep, came]), jnp.stack([came, keep]))

    small = jnp.concatenate(
        [part.astype(F32).reshape(-1) for part in (token_ids, modality, loss_mask, targets, gains)]
    )[None]
    small = jnp.concatenate([small, flip(small, PAIR)])
    local_first, small = tie(local_first, small)
    masks = [0, PAIR]
    for bit in high_bits + [1]:
        small = jnp.concatenate([small, flip(small, bit)])
        masks = masks + [mask | bit for mask in masks]
    order = blk ^ jnp.arange(blocks)
    mine_first = paired(*sides_of(local_first))
    small = small[jnp.array([masks.index(mask) for mask in range(blocks)])[order]]
    cells = clips * span
    ids_all, modality_all, mask_all, targets_all = (
        small[:, k * cells : (k + 1) * cells]
        .astype(jnp.int32)
        .reshape(blocks, clips, span)
        .transpose(1, 0, 2)
        .reshape(clips, length)
        for k in range(4)
    )
    gains_full = small[:, 4 * cells :].reshape(blocks, 3, rows).transpose(1, 0, 2).reshape(3, D)

    def spread_high(mine, at=slice(None)):
        pieces = [mine[at]]
        for bit in high_bits:
            pieces = pieces + [flip(piece, bit) for piece in pieces]
        return tuple(pieces[1:])

    def both_sides(first, second):
        return tuple(jnp.stack(pair) for pair in zip(first, second))

    def spread_low(pieces):
        return tuple(flip(piece, 1) for piece in pieces)

    def assembled(mine, far, near):
        pieces = (mine, *far, *near)
        places = [high ^ (k % highs) if side_at == 0 else low ^ (k // highs)
                  for k in range(len(pieces)) for side_at in range(2)]
        return assembled_at(jnp.stack(places).astype(jnp.int32), pieces)

    mine = [mine_first, None, None, None]
    far = [None] * 4
    near = [None] * 4

    head_order = ((core ^ jnp.arange(2))[:, None] * ys + (y_at ^ jnp.arange(ys))[None]).reshape(-1)

    def by_device(array):
        split = array.reshape(highs, 2, 2, 2, ys, own).transpose(0, 3, 1, 2, 4, 5)
        split = split.reshape(blocks, 2 * ys, own)[:, head_order]
        return split.reshape(blocks, half)

    image_rows = image_table.shape[0]
    code_local = code_table.shape[0]
    table = jnp.concatenate([image_table.astype(HALF), code_table.astype(HALF)])
    ids_dev, modality_dev = by_device(ids_all)[order], by_device(modality_all)[order]
    code_rows = jnp.clip(jnp.where(modality_dev == 1, ids_dev, VT + ids_dev), 0, VT + VA - 1)
    image_at = ids_dev - blk * image_rows
    code_at = code_rows - blk * code_local
    image_at = jnp.where((image_at >= 0) & (image_at < image_rows), image_at, -1)
    code_at = jnp.where((code_at >= 0) & (code_at < code_local), code_at + image_rows, -1)
    table_at = jnp.where(modality_dev == 0, image_at, code_at)
    table_rows = image_rows + code_local
    pick = (table_at.reshape(-1)[:, None] == jnp.arange(table_rows)[None, :]).astype(HALF)
    picked = dot(pick, table, ((1,), (0,)), HALF)
    width = table.shape[1]
    levels = len(all_bits)
    picked = picked.reshape((2,) * levels + (half, width))

    def token_hop(part, bit, left):
        axis = left.index(bit)
        keep = lax.index_in_dim(part, 0, axis, keepdims=False)
        send = lax.index_in_dim(part, 1, axis, keepdims=False)
        return keep + flip(send, bit)

    left = sorted(all_bits, reverse=True)
    mid = 3 * width // 4
    picked, mine[0] = tie(picked, mine[0])
    far[0] = spread_high(mine[0])
    part_a = token_hop(picked[..., :mid], 1, left)
    part_b = token_hop(picked[..., mid:], PAIR, left)
    local[1:] = [sides_of(halves) for halves in local[1:]]
    part_a = token_hop(part_a, PAIR, left[:-1])
    part_b = token_hop(part_b, 1, left[:-2] + left[-1:])
    part_a, part_b, mine[0], far[0], local[1] = tie(part_a, part_b, mine[0], far[0], local[1])
    mine[1] = paired(*local[1])
    near_own = spread_low(mine[:1])
    for k, bit in enumerate(high_bits[::-1]):
        part_a = token_hop(part_a, bit, left[k:-2])
        part_b = token_hop(part_b, bit, left[k:-2])
    block = jnp.concatenate([part_a, part_b], axis=-1)
    block, mine[1], far[0], near_own, local[2:] = tie(block, mine[1], far[0], near_own, local[2:])
    far_side, near_far = spread_high(mine[1], 0), spread_low(far[0])
    of_core = [
        [block if not bits else hop(block, *bits) for bits in row]
        for row in ([()] + near_peers[: ys - 1], near_peers[ys - 1 :])
    ]
    of_core, far_side, near_far, mine[1], local[2] = tie(
        of_core, far_side, near_far, mine[1], local[2]
    )
    near[0] = (*near_own, *near_far)
    far_other, near_own = spread_high(mine[1], 1), spread_low(mine[1:2])
    mine[2] = paired(*local[2])
    column_pieces = [[row, [hop(piece, 0, 1) for piece in row]] for row in of_core]
    column_at = jnp.stack([head ^ (2 * y + c) for c in range(2) for y in range(ys)])
    normed_in, embedded_own = joined_norm(column_pieces, column_at, gains_full[0], own)
    w_first = assembled(mine[0], far[0], near[0])
    head_columns = w_first.shape[-1] // 4
    w_in, w_out = w_first[:, : 3 * head_columns], w_first[:, 3 * head_columns :]
    local_heads = head_columns // HD
    mixed = dot(normed_in, w_in, ((1,), (0,)), HALF)
    mixed, near_own, far_other, mine[2], local[3] = tie(
        mixed, near_own, far_other, mine[2], local[3]
    )
    mine[3] = paired(*local[3])
    far[1] = both_sides(far_side, far_other)
    far_side = spread_high(mine[2], 0)
    block_order = (
        ((core ^ jnp.arange(2))[:, None, None] * 2 + (side ^ jnp.arange(2))[None, :, None]) * ys
        + (y_at ^ jnp.arange(ys))[None, None]
    ).reshape(-1)
    query_pos = place * team + (block_order[:, None] * own + jnp.arange(own)[None]).reshape(-1)
    query_pos = query_pos.astype(jnp.int32)

    def key_pos(back):
        return jnp.where(query_pos >= back * team, query_pos - back * team, length)

    pairs_own = mixed[:, head_columns:]
    earlier = [lax.ppermute(pairs_own, "blk", index_of(back)) for back in range(1, per_clip)]
    running = attend(
        mixed, mixed, local_heads, query_pos, query_pos, (), per_clip == 1, local_heads
    )
    running, earlier, far_side, far[1], mine[2], mine[3] = tie(
        running, earlier, far_side, far[1], mine[2], mine[3]
    )
    far_other, near_far = spread_high(mine[2], 1), spread_low(far[1])
    for back in range(1, per_clip):
        running = attend(
            mixed,
            earlier[back - 1],
            0,
            query_pos,
            key_pos(back),
            running,
            back == per_clip - 1,
            local_heads,
        )
    flat_heads, log_total = running
    made = core_sum(flat_heads[:half], flat_heads[half:], w_out, ((1,), (1,)))
    made, mine[2] = tie(made, mine[2])
    near_next = spread_low(mine[2:3])
    first, near_far, far_other = group_sum(made, near_far, far_other)
    near[1] = (*near_own, *near_far)
    w_up = assembled(mine[1], far[1], near[1])
    first = embedded_own + first
    far[2] = both_sides(far_side, far_other)
    far_side, near_far = spread_high(mine[3], 0), spread_low(far[2])
    normed_mid, far_side, near_far, near_next, w_up, mine[3] = gathered(
        rms_norm(first, gains_full[1]).astype(HALF), far_side, near_far, near_next, w_up, mine[3]
    )
    near[2] = (*near_next, *near_far)
    w_down = assembled(mine[2], far[2], near[2])
    hidden_up = [dot(part, w_up, ((1,), (0,))) for part in normed_mid]
    active = [jax.nn.gelu(part).astype(HALF) for part in hidden_up]
    near_own, far_other = spread_low(mine[3:]), spread_high(mine[3], 1)
    made = core_sum(*active, w_down, ((1,), (1,)))
    second, near_own, far_other = group_sum(made, near_own, far_other)
    far[3] = both_sides(far_side, far_other)
    second = first + second
    final_in, *near_far = gathered(
        rms_norm(second, gains_full[2]).astype(HALF), *spread_low(far[3])
    )
    w_read = assembled(mine[3], far[3], (*near_own, *near_far))
    logits = [dot(part, w_read, ((1,), (0,))) for part in final_in]

    def of_team(array):
        taken = lax.dynamic_slice(array, (clip, place * team), (1, team))
        return taken.reshape(ranks, own)[block_order].reshape(team)

    weight_all = (
        (mask_all == 1) & (jnp.arange(length)[None, :] < clip_lengths[:, None])
    ).astype(F32)
    loss_count = jnp.sum(weight_all)
    weight_of = of_team(weight_all)
    targets_own = of_team(targets_all)
    vocab_local = logits[0].shape[1]
    column_ids = (head * 2 + side) * vocab_local + jnp.arange(vocab_local)
    halves = (slice(0, half), slice(half, team))
    match = [column_ids[None, :] == targets_own[at][:, None] for at in halves]
    parts = []
    for part, hit in zip(logits, match):
        top = jnp.max(part, axis=-1)
        total = jnp.sum(jnp.exp(part - top[:, None]), axis=-1)
        parts.append(jnp.stack([top, total, jnp.sum(jnp.where(hit, part, 0.0), axis=-1)]))
    stats = jnp.concatenate(parts, axis=1)
    for axis, bits in [(2, (PAIR, 0)), (1, (0, 1))] + [
        (3, (0, 2 << k)) for k in range(ys.bit_length() - 1)
    ]:
        other = hop(stats, *bits).reshape(3, 2, 2, ys, own)
        flipped = np.arange(other.shape[axis]) ^ (bits[1] // 2 if axis == 3 else 1)
        other = jnp.stack(
            [lax.index_in_dim(other, k, axis, keepdims=False) for k in flipped], axis=axis
        ).reshape(3, team)
        top = jnp.maximum(stats[0], other[0])
        total = stats[1] * jnp.exp(stats[0] - top) + other[1] * jnp.exp(other[0] - top)
        stats = jnp.stack([top, total, stats[2] + other[2]])
    log_norm = stats[0] + jnp.log(stats[1])
    per_token = (log_norm + ZCOEF * log_norm * log_norm - stats[2]) * weight_of
    loss_part = jnp.sum(per_token) * (rank == 0).astype(F32)

    token_grad = weight_of / loss_count
    grad_logits = []
    for part, hit, at in zip(logits, match, halves):
        probs = jnp.exp(part - log_norm[at][:, None])
        scaled = probs * (1.0 + 2.0 * ZCOEF * log_norm[at])[:, None] - hit.astype(F32)
        grad_logits.append((token_grad[at][:, None] * scaled).astype(HALF))

    top_bit = high_bits[-1]
    top = (blk // top_bit) % 2

    def made_of(left, right):
        return dot(left, right, ((0,), (0,)), HALF).reshape(
            2, highs // 2, 2, 2, rows, right.shape[1]
        )

    def low_part(made, at_top, at_low):
        chosen = lax.dynamic_index_in_dim(made, at_top, 0, keepdims=False)
        return lax.dynamic_index_in_dim(chosen, at_low, 2, keepdims=False)

    def send_low(made, at_top):
        return flip(low_part(made, at_top, 1 - low), 1)

    def add_low(made, at_top, came):
        return low_part(made, at_top, low).astype(F32) + came.astype(F32)

    def for_top(made, came):
        total = add_low(made, 1 - top, came).astype(HALF)
        return total[:, 0], total[:, 1]

    def send_high(part):
        return flip(part, top_bit)

    def add_high(made, came_low, came_high):
        total = add_low(made, top, came_low) + jnp.stack(came_high, axis=1).astype(F32)
        total = total.reshape((2,) * (len(high_bits) - 1) + total.shape[1:])
        for bit in high_bits[-2::-1] if len(high_bits) > 1 else []:
            at = (blk // bit) % 2
            send = lax.dynamic_index_in_dim(total, 1 - at, 0, keepdims=False)
            keep = lax.dynamic_index_in_dim(total, at, 0, keepdims=False)
            total = keep + flip(send.astype(HALF), bit).astype(F32)
        return total

    def sum_sides(total):
        send = lax.dynamic_index_in_dim(total, 1 - side, 0, keepdims=False)
        keep = lax.dynamic_index_in_dim(total, side, 0, keepdims=False)
        came = flip(send.astype(HALF), PAIR).astype(F32)
        return jnp.where(side == 0, keep, came), jnp.where(side == 0, came, keep)

    def joined(parts):
        return jnp.concatenate(parts)

    made = core_sum(*grad_logits, w_read, ((1,), (1,)))
    made, read_made = tie(made, made_of(joined(final_in), joined(grad_logits)))
    read_far = send_low(read_made, 1 - top)
    grad_final, read_made, read_far = group_sum(made, read_made, read_far)
    read_near = send_low(read_made, top)
    read_top = for_top(read_made, read_far)
    read_first = send_high(read_top[0])
    grad_second, gain_final = norm_back(second, gains_full[2], grad_final)
    branch_grad, read_near, read_first, read_top = gathered(
        grad_second.astype(HALF), read_near, read_first, read_top
    )
    read_second = send_high(read_top[1])
    grad_hidden = []
    for part, up in zip(branch_grad, hidden_up):
        unused_gelu, gelu_pull = jax.vjp(jax.nn.gelu, up)
        grad_hidden.append(gelu_pull(dot(part, w_down, ((1,), (0,))))[0].astype(HALF))
    made = core_sum(*grad_hidden, w_up, ((1,), (1,)))
    made, normed_mid, grad_hidden, read_second, down_made = tie(
        made,
        normed_mid,
        grad_hidden,
        read_second,
        made_of(joined(branch_grad), joined(active)),
    )
    read_total = add_high(read_made, read_near, (read_first, read_second))
    down_far = send_low(down_made, 1 - top)
    grad_mid, down_made, down_far, up_made = group_sum(
        made, down_made, down_far, made_of(joined(normed_mid), joined(grad_hidden))
    )
    down_near = send_low(down_made, top)
    down_top = for_top(down_made, down_far)
    down_first = send_high(down_top[0])
    grad_mid_in, gain_mid = norm_back(first, gains_full[1], grad_mid)
    grad_first = grad_second + grad_mid_in
    attn_grad, up_made, down_near, down_first, down_top, read_total = gathered(
        grad_first.astype(HALF), up_made, down_near, down_first, down_top, read_total
    )
    down_second = send_high(down_top[1])
    up_far = send_low(up_made, 1 - top)
    attn_grad = joined(attn_grad)
    grad_heads = dot(attn_grad, w_out, ((1,), (0,)), HALF)
    returned = []
    grad_query = None
    for back in range(1, per_clip):
        grad_query, far_pairs = attend_back(
            mixed,
            earlier[back - 1],
            0,
            query_pos,
            key_pos(back),
            flat_heads,
            grad_heads,
            log_total,
            grad_query,
            False,
            local_heads,
        )
        if back == 1:
            far_pairs, up_made, up_far, down_second, read_total = tie(
                far_pairs, up_made, up_far, down_second, read_total
            )
            grad_read = sum_sides(read_total)
            grad_down = sum_sides(add_high(down_made, down_near, (down_first, down_second)))
            up_near = send_low(up_made, top)
            up_top = for_top(up_made, up_far)
            up_first = send_high(up_top[0])
        returned.append(lax.ppermute(far_pairs, "blk", index_of(-back)))
    grad_query, grad_pairs = attend_back(
        mixed,
        mixed,
        local_heads,
        query_pos,
        query_pos,
        flat_heads,
        grad_heads,
        log_total,
        grad_query,
        True,
        local_heads,
    )
    for far_pairs in returned:
        grad_pairs = grad_pairs + far_pairs.astype(F32)
    grad_mixed = jnp.concatenate([grad_query, grad_pairs.astype(HALF)], axis=1)
    grad_mixed, up_first, up_top, grad_read = tie(grad_mixed, up_first, up_top, grad_read)
    up_second = send_high(up_top[1])
    made = core_sum(grad_mixed[:half], grad_mixed[half:], w_in, ((1,), (1,)))
    made, in_made, out_made, up_near, grad_down = tie(
        made,
        made_of(normed_in, grad_mixed),
        made_of(attn_grad, flat_heads),
        up_near,
        grad_down,
    )
    in_far, out_far = send_low(in_made, 1 - top), send_low(out_made, 1 - top)
    grad_norm_in, in_made, out_made, in_far, out_far, up_second = group_sum(
        made, in_made, out_made, in_far, out_far, up_second
    )
    in_near, out_near = send_low(in_made, top), send_low(out_made, top)
    in_top, out_top = for_top(in_made, in_far), for_top(out_made, out_far)
    in_first, out_first = send_high(in_top[0]), send_high(out_top[0])
    grad_embed_in, gain_in = norm_back(embedded_own, gains_full[0], grad_norm_in)
    grad_embed = (grad_first + grad_embed_in).astype(HALF)

    def columns_of(head_bits):
        at = (head ^ head_bits) * width
        return lax.dynamic_slice(grad_embed, (0, at), (own, width))

    head_bits = [2 * y + c for c in range(2) for y in range(ys)]
    head_parts = [
        columns_of(bits) if bits == 0 else hop(columns_of(bits), 0, bits) for bits in head_bits
    ]
    grad_up = sum_sides(add_high(up_made, up_near, (up_first, up_second)))
    columns_own = jnp.concatenate(head_parts)
    gain_own = jnp.stack([gain_in, gain_mid, gain_final])
    for k in range(heads.bit_length() - 1):
        gain_own = gain_own + hop(gain_own, 0, 1 << k)

    def spread(pieces, bit):
        return jnp.concatenate([pieces, flip(pieces, bit)])

    mid = width // 2
    gain_rows = gain_own.astype(HALF).reshape(-1, width - mid)
    gain_rows = jnp.pad(gain_rows, ((0, -gain_rows.shape[0] % 16), (0, 0)))
    pieces_a, pieces_b = tie(
        columns_own[None, :, :mid], jnp.concatenate([columns_own[:, mid:], gain_rows])[None]
    )
    for bit in high_bits[::-1]:
        pieces_a, pieces_b = spread(pieces_a, bit), spread(pieces_b, bit)
    pieces_a, pieces_b, in_first, out_first, in_top, out_top, in_near, out_near = tie(
        pieces_a, pieces_b, in_first, out_first, in_top, out_top, in_near, out_near
    )
    in_second, out_second = send_high(in_top[1]), send_high(out_top[1])
    pieces_a, pieces_b = spread(pieces_a, PAIR), spread(pieces_b, 1)
    pieces_a, pieces_b, in_second, out_second, grad_up = tie(
        pieces_a, pieces_b, in_second, out_second, grad_up
    )
    pieces = (pieces_a, flip(pieces_a, 1), pieces_b, flip(pieces_b, PAIR))
    pieces, in_total, out_total = tie(
        pieces,
        add_high(in_made, in_near, (in_first, in_second)),
        add_high(out_made, out_near, (out_first, out_second)),
    )
    grad_in, grad_out_w = sum_sides(in_total), sum_sides(out_total)
    gain_sum = sum(jnp.sum(part[:, half:].astype(F32), axis=0) for part in pieces[2:])
    gain_sum = gain_sum.reshape(-1)[: 3 * D].reshape(3, D)
    gain_sum = lax.dynamic_slice_in_dim(gain_sum, blk * rows, rows, 1)
    masks_a, masks_b = [0], [0]
    for bit_a, bit_b in zip(high_bits[::-1] + [PAIR, 1], high_bits[::-1] + [1, PAIR]):
        masks_a = masks_a + [mask | bit_a for mask in masks_a]
        masks_b = masks_b + [mask | bit_b for mask in masks_b]
    places = [[masks.index(mask) for mask in range(blocks)] for masks in (masks_a, masks_b)]
    row_step = max(s for s in range(8, 321, 8) if table_rows % s == 0)
    grad_table = table_grad(table_at, pieces, places, table_rows, row_step)
    img_sum, code_sum = grad_table[:image_rows], grad_table[image_rows:]

    in_sum = jnp.stack(
        [
            jnp.concatenate(
                [part[:, k * head_columns : (k + 1) * head_columns] for part in grad_in], axis=1
            )
            for k in range(3)
        ]
    )
    out_sum = jnp.concatenate([part.T for part in grad_out_w])
    down_sum = jnp.concatenate([part.T for part in grad_down])
    up_sum = jnp.concatenate(grad_up, axis=1)
    read_sum = jnp.concatenate(grad_read, axis=1)
    in_sum, out_sum, up_sum, down_sum, read_sum = (
        with_layout_constraint(total, Layout(major_to_minor=tuple(range(total.ndim))))
        for total in (in_sum, out_sum, up_sum, down_sum, read_sum)
    )
    sums = [in_sum, out_sum, up_sum, down_sum, img_sum, code_sum, read_sum, gain_sum]
    local_squares = jnp.float32(0.0)
    for shard in sums[:7]:
        local_squares = local_squares + jnp.sum(shard * shard)
    local_squares = local_squares + (head == 0).astype(F32) * jnp.sum(gain_sum * gain_sum)
    mine = jnp.broadcast_to(
        jnp.stack([local_squares, loss_part])[None, :, None], (blocks * heads, 2, 128)
    )
    totals = jnp.sum(lax.all_to_all(mine, both, 0, 0, tiled=True), axis=0)
    grad_norm = jnp.sqrt(totals[0, 0])
    loss_sum = totals[1, 0]
    factor = jnp.minimum(1.0, CLIP / grad_norm)
    spreads = [
        D ** (-0.5),
        (length // 2) ** 0.5 * D ** (-0.5),
        D ** (-0.5),
        FF ** (-0.5),
        0.05,
        0.05,
        2.0 * D ** (-0.5),
    ]
    weights = [inward, outward, expand, contract, image_table, code_table, readout, gains]
    firsts = [
        inward_first,
        outward_first,
        expand_first,
        contract_first,
        image_first,
        code_first,
        readout_first,
        gains_first,
    ]
    seconds = [
        inward_second,
        outward_second,
        expand_second,
        contract_second,
        image_second,
        code_second,
        readout_second,
        gains_second,
    ]
    result = []
    for index in range(8):
        rate = GAIN_RATE if index == 7 else RATE_FACTOR * spreads[index]
        decay = 0.0 if index == 7 else DECAY
        result.extend(
            adamw(weights[index], firsts[index], seconds[index], sums[index] * factor, rate, decay)
        )
    return (*result, loss_sum, loss_count, grad_norm)


def solution(mesh):
    matrices = (
        P(None, "blk", "head"),
        P("head", "blk"),
        P("blk", "head"),
        P("head", "blk"),
        P("blk", "head"),
        P("blk", "head"),
        P("blk", "head"),
        P(None, "blk"),
    )
    tokens = P(None, "blk")
    return jax.shard_map(
        shards,
        mesh=mesh,
        in_specs=matrices * 3 + (tokens, tokens, P(), tokens, tokens),
        out_specs=tuple(spec for spec in matrices for _ in range(3)) + (P(), P(), P()),
        check_vma=False,
    )
```

```python
import jax
import jax.numpy as jnp
import numpy as np
from jax import lax
from jax.experimental import pallas as pl
from jax.experimental.layout import Layout, with_layout_constraint
from jax.experimental.pallas import tpu as pltpu
from jax.sharding import PartitionSpec as P

D = 2048
HD = 128
FF = 8192
VT = 1024
VA = 256
STEP = 10


EPS = 1e-05
ZCOEF = 0.01
CLIP = 0.02
BETA1 = 0.9
BETA2 = 0.95
ADAM_EPS = 1e-08
DECAY = 0.1
RATE_FACTOR = 1.5
GAIN_RATE = 0.8

HALF = jnp.bfloat16
F32 = jnp.float32
NEG = -1e30
LOG2E = 1.4426950408889634
SCORE = HD ** (-0.5) * LOG2E
PAIR = 2


def flip(value, bit):
    count = lax.axis_size("blk")
    return lax.ppermute(value, "blk", [(i, i ^ bit) for i in range(count)])


def rms_norm(hidden, gain):
    return hidden * lax.rsqrt(jnp.mean(hidden * hidden, axis=-1, keepdims=True) + EPS) * gain


def norm_back(hidden, gain, upstream):
    unused, pullback = jax.vjp(rms_norm, hidden, gain)
    return pullback(upstream)


def dot(left, right, dims, out=F32):
    return lax.dot_general(left, right, (dims, ((), ())), preferred_element_type=F32).astype(out)


def adamw(weight, first, second, grad, rate, decay):
    first = BETA1 * first + (1.0 - BETA1) * grad
    second = BETA2 * second + (1.0 - BETA2) * grad * grad
    first_hat = first / (1.0 - BETA1**STEP)
    second_hat = second / (1.0 - BETA2**STEP)
    weight = weight - rate * (first_hat / (jnp.sqrt(second_hat) + ADAM_EPS) + decay * weight)
    return (weight, first, second)


def dot_last(left, right):
    return lax.dot_general(left, right, (((1,), (1,)), ((), ())), preferred_element_type=F32)


def dot_first(left, right):
    return lax.dot_general(left, right, (((0,), (0,)), ((), ())), preferred_element_type=F32)


def attend_kernel(opening, closing, qpos_ref, kpos_ref, q_ref, k_ref, v_ref, *refs):
    scores = dot_last(k_ref[...], q_ref[...]) * SCORE
    scores = jnp.where(kpos_ref[...] <= qpos_ref[...], scores, NEG)
    top = jnp.max(scores, axis=0, keepdims=True)
    if not opening:
        acc_in, top_in, total_in = refs[:3]
        refs = refs[3:]
        top = jnp.maximum(top, top_in[0])
    weights = jnp.exp2(scores - top)
    total = jnp.sum(weights, axis=0, keepdims=True)
    acc = dot_first(v_ref[...], weights.astype(HALF))
    if not opening:
        fading = jnp.exp2(top_in[0] - top)
        total = total + total_in[0] * fading
        acc = acc + acc_in[0] * fading
    if closing:
        out_ref, log_ref = refs
        out_ref[...] = (acc / total).T.astype(HALF)
        log_ref[0] = top + jnp.log2(total)
    else:
        acc_ref, top_ref, total_ref = refs
        acc_ref[0] = acc
        top_ref[0] = top
        total_ref[0] = total


def attend(queries, pairs, at, query_pos, key_pos, state, closing, count):
    team = queries.shape[0]
    step = min(team, 256)
    row = pl.BlockSpec((1, 1, step), lambda h, i: (h, 0, i))
    wide = pl.BlockSpec((1, HD, step), lambda h, i: (h, 0, i))
    rows = jax.ShapeDtypeStruct((count, 1, team), F32)
    if closing:
        out_specs = [pl.BlockSpec((step, HD), lambda h, i: (i, h)), row]
        out_shape = [jax.ShapeDtypeStruct((team, count * HD), HALF), rows]
    else:
        out_specs = [wide, row, row]
        out_shape = [jax.ShapeDtypeStruct((count, HD, team), F32), rows, rows]
    return pl.pallas_call(
        lambda *refs: attend_kernel(not state, closing, *refs),
        grid=(count, team // step),
        in_specs=[
            pl.BlockSpec((1, step), lambda h, i: (0, i)),
            pl.BlockSpec((team, 1), lambda h, i: (0, 0)),
            pl.BlockSpec((step, HD), lambda h, i: (i, h)),
            pl.BlockSpec((team, HD), lambda h, i: (0, at + h)),
            pl.BlockSpec((team, HD), lambda h, i: (0, at + count + h)),
        ]
        + ([wide, row, row] if state else []),
        out_specs=out_specs,
        out_shape=out_shape,
        compiler_params=pltpu.CompilerParams(vmem_limit_bytes=40 * 2**20),
        cost_estimate=pl.CostEstimate(
            flops=4 * count * team * team * HD,
            bytes_accessed=10 * count * team * HD,
            transcendentals=count * team * team,
        ),
    )(query_pos[None], key_pos[:, None], queries, pairs, pairs, *state)


def attend_back_kernel(opening, closing, qpos_ref, kpos_ref, q_ref, k_ref, v_ref, *refs):
    out_ref, grad_ref, log_ref = refs[:3]
    query_in, (query_ref, pair_ref, keys_acc, values_acc) = refs[3:-4], refs[-4:]
    head, step = pl.program_id(0), pl.program_id(1)
    grad = grad_ref[...]
    inner = (grad.astype(F32) * out_ref[...].astype(F32)).T
    inner = jnp.sum(inner, axis=0, keepdims=True)
    scores = dot_last(k_ref[...], q_ref[...]) * SCORE
    seen = kpos_ref[...] <= qpos_ref[...]
    probs = jnp.where(seen, jnp.exp2(scores - log_ref[0]), 0.0)
    grad_probs = dot_last(v_ref[...], grad)
    grad_scores = (probs * (grad_probs - inner)).astype(HALF)
    grad_query = dot_first(k_ref[...], grad_scores)
    if not opening:
        grad_query = grad_query + query_in[0][0]
    if closing:
        query_ref[...] = (grad_query * HD ** (-0.5)).T.astype(HALF)
    else:
        query_ref[0] = grad_query

    @pl.when(step == 0)
    def clear():
        keys_acc[...] = jnp.zeros_like(keys_acc)
        values_acc[...] = jnp.zeros_like(values_acc)

    keys_acc[...] += jnp.dot(grad_scores, q_ref[...], preferred_element_type=F32)
    values_acc[...] += jnp.dot(probs.astype(HALF), grad, preferred_element_type=F32)

    @pl.when(step == pl.num_programs(1) - 1)
    def write():
        half = pair_ref.shape[1] // 2
        at = pl.multiple_of(head * HD, HD)
        pair_ref[:, pl.ds(at, HD)] = (keys_acc[...] * HD ** (-0.5)).astype(pair_ref.dtype)
        pair_ref[:, pl.ds(half + at, HD)] = values_acc[...].astype(pair_ref.dtype)


def attend_back(queries, pairs, at, query_pos, key_pos, out, grad, log_total, state, closing, count):
    team = queries.shape[0]
    step = min(team, 256)
    wide = pl.BlockSpec((1, HD, step), lambda h, i: (h, 0, i))
    block = pl.BlockSpec((step, HD), lambda h, i: (i, h))
    if closing:
        query_spec, query_shape = block, jax.ShapeDtypeStruct((team, count * HD), HALF)
    else:
        query_spec, query_shape = wide, jax.ShapeDtypeStruct((count, HD, team), F32)
    return pl.pallas_call(
        lambda *refs: attend_back_kernel(state is None, closing, *refs),
        grid=(count, team // step),
        in_specs=[
            pl.BlockSpec((1, step), lambda h, i: (0, i)),
            pl.BlockSpec((team, 1), lambda h, i: (0, 0)),
            block,
            pl.BlockSpec((team, HD), lambda h, i: (0, at + h)),
            pl.BlockSpec((team, HD), lambda h, i: (0, at + count + h)),
            block,
            block,
            pl.BlockSpec((1, 1, step), lambda h, i: (h, 0, i)),
        ]
        + ([] if state is None else [wide]),
        out_specs=[query_spec, pl.BlockSpec((team, 2 * count * HD), lambda h, i: (0, 0))],
        out_shape=[
            query_shape,
            jax.ShapeDtypeStruct((team, 2 * count * HD), F32 if closing else HALF),
        ],
        scratch_shapes=[pltpu.VMEM((team, HD), F32), pltpu.VMEM((team, HD), F32)],
        compiler_params=pltpu.CompilerParams(vmem_limit_bytes=48 * 2**20),
        cost_estimate=pl.CostEstimate(
            flops=10 * count * team * team * HD,
            bytes_accessed=20 * count * team * HD,
            transcendentals=count * team * team,
        ),
    )(
        query_pos[None],
        key_pos[:, None],
        queries,
        pairs,
        pairs,
        out,
        grad,
        log_total,
        *([] if state is None else [state]),
    )


def joined_norm_kernel(sides, at_ref, gain_ref, *refs):
    pieces, out_ref, first_ref = refs[:-2], refs[-2], refs[-1]
    count = len(pieces) // sides
    width = pieces[0].shape[1]
    is_first = (pl.program_id(0) == 0) & (pl.program_id(1) == 0)
    for side in range(sides):
        parts = [ref[...].astype(F32) for ref in pieces[side * count : (side + 1) * count]]
        squares = sum(jnp.sum(part * part, axis=-1, keepdims=True) for part in parts)
        scale = lax.rsqrt(squares / (count * width) + EPS)
        for k, part in enumerate(parts):
            at = pl.ds(pl.multiple_of(at_ref[k] * width, width), width)
            out_ref[0, side, 0, :, at] = (part * scale * gain_ref[:, at]).astype(HALF)
            if side == 0:

                @pl.when(is_first)
                def keep():
                    first_ref[:, at] = part


def joined_norm(pieces, at, gain, own):
    ys = len(pieces[0][0])
    width = pieces[0][0][0].shape[1]
    columns = 2 * ys * width
    flat, specs = [], []
    for of_side in pieces:
        for core, of_core in enumerate(of_side):
            for y, piece in enumerate(of_core):
                flat.append(piece)
                specs.append(
                    pl.BlockSpec(
                        (own, width),
                        lambda c, k, at, core=core, y=y: ((c ^ core) * ys + (k ^ y), 0),
                    )
                )
    grid = pltpu.PrefetchScalarGridSpec(
        num_scalar_prefetch=1,
        grid=(2, ys),
        in_specs=[pl.BlockSpec((1, columns), lambda c, k, at: (0, 0))] + specs,
        out_specs=[
            pl.BlockSpec((1, 2, 1, own, columns), lambda c, k, at: (c, 0, k, 0, 0)),
            pl.BlockSpec((own, columns), lambda c, k, at: (0, 0)),
        ],
    )
    normed, first = pl.pallas_call(
        lambda *refs: joined_norm_kernel(2, *refs),
        grid_spec=grid,
        out_shape=[
            jax.ShapeDtypeStruct((2, 2, ys, own, columns), HALF),
            jax.ShapeDtypeStruct((own, columns), F32),
        ],
        compiler_params=pltpu.CompilerParams(vmem_limit_bytes=60 * 2**20),
        cost_estimate=pl.CostEstimate(
            flops=20 * ys * own * columns, bytes_accessed=16 * ys * own * columns, transcendentals=0
        ),
    )(at, gain[None], *flat)
    return normed.reshape(4 * ys * own, columns), first


def table_grad_kernel(places, at_ref, *refs):
    parts, out_ref = refs[:-1], refs[-1]
    tokens = at_ref.shape[1]
    width = parts[0].shape[2]
    step = out_ref.shape[0]
    row = pl.program_id(0) * step + lax.broadcasted_iota(jnp.int32, (step, tokens), 0)
    for part, order in enumerate(places):
        total = jnp.zeros((step, width), F32)
        for k, place in enumerate(order):
            pieces, at = parts[2 * part + place // (len(order) // 2)], place % (len(order) // 2)
            pick = (row == at_ref[k][None, :]).astype(F32).astype(HALF)
            total += jnp.dot(pick, pieces[at, :tokens], preferred_element_type=F32)
        out_ref[:, part * width : (part + 1) * width] = total


def table_grad(at, parts, places, rows, step):
    count, tokens = at.shape
    columns = parts[0].shape[2] * len(places)
    return pl.pallas_call(
        lambda *refs: table_grad_kernel(places, *refs),
        grid=(rows // step,),
        in_specs=[pl.BlockSpec((count, tokens), lambda i: (0, 0))]
        + [pl.BlockSpec(part.shape, lambda i: (0, 0, 0)) for part in parts],
        out_specs=pl.BlockSpec((step, columns), lambda i: (i, 0)),
        out_shape=jax.ShapeDtypeStruct((rows, columns), F32),
        compiler_params=pltpu.CompilerParams(vmem_limit_bytes=56 * 2**20),
        cost_estimate=pl.CostEstimate(
            flops=2 * rows * count * tokens * columns,
            bytes_accessed=2 * count * tokens * columns + 4 * rows * columns,
            transcendentals=0,
        ),
    )(at, *parts)


def assembled_kernel(count, at_ref, *refs):
    pieces, out_ref = refs[:count], refs[count]
    for k, piece in enumerate(pieces):

        @pl.when(pl.program_id(0) == k)
        def write():
            out_ref[0, :, 0] = piece[...]


def assembled_at(places, pieces, grant):
    count = len(pieces)
    unused, rows, columns = pieces[0].shape
    grid = pltpu.PrefetchScalarGridSpec(
        num_scalar_prefetch=1,
        grid=(count,),
        in_specs=[pl.BlockSpec((2, rows, columns), lambda i, at: (0, 0, 0)) for piece in pieces],
        out_specs=pl.BlockSpec(
            (1, 2, 1, rows, columns), lambda i, at: (at[2 * i], 0, at[2 * i + 1], 0, 0)
        ),
    )
    whole = pl.pallas_call(
        lambda *refs: assembled_kernel(count, *refs),
        grid_spec=grid,
        out_shape=jax.ShapeDtypeStruct((count // 2, 2, 2, rows, columns), HALF),
        compiler_params=pltpu.CompilerParams(vmem_limit_bytes=grant * 2**20),
        cost_estimate=pl.CostEstimate(
            flops=0, bytes_accessed=4 * count * pieces[0].size, transcendentals=0
        ),
    )(places, *pieces)
    return whole.reshape(count * 2 * rows, columns)


def shards(
    inward,
    outward,
    expand,
    contract,
    image_table,
    code_table,
    readout,
    gains,
    inward_first,
    outward_first,
    expand_first,
    contract_first,
    image_first,
    code_first,
    readout_first,
    gains_first,
    inward_second,
    outward_second,
    expand_second,
    contract_second,
    image_second,
    code_second,
    readout_second,
    gains_second,
    token_ids,
    modality,
    clip_lengths,
    loss_mask,
    targets,
):
    blocks = lax.axis_size("blk")
    heads = lax.axis_size("head")
    blk = lax.axis_index("blk")
    head = lax.axis_index("head")
    clips, span = token_ids.shape
    length = span * blocks
    rows = D // blocks
    low = blk % 2
    side = (blk // 2) % 2
    high = blk // 4
    highs = blocks // 4
    groups = blocks // 2
    group = high * 2 + low
    per_clip = groups // clips
    clip = group // per_clip
    place = group % per_clip
    ranks = 2 * heads
    core, y_at, ys = head % 2, head // 2, heads // 2
    rank = side * heads + head
    team = clips * length // groups
    half = team // 2
    own = team // ranks
    high_bits = [1 << k for k in range(2, blocks.bit_length() - 1)]
    all_bits = [1, 2] + high_bits
    both = ("blk", "head")
    near_peers = [(side_bit, 2 * y) for side_bit in (0, PAIR) for y in range(ys)][1:]

    def hop(value, blk_bits, head_bits):
        pairs = [
            (i * heads + h, (i ^ blk_bits) * heads + (h ^ head_bits))
            for i in range(blocks)
            for h in range(heads)
        ]
        return lax.ppermute(value, both, pairs)

    def tie(*values):
        return lax.optimization_barrier(values)

    def gathered(block, *riders):
        parts, riders = tie([hop(block, *bits) for bits in near_peers], riders)
        mine = jnp.concatenate([block] + parts)
        return ((mine, hop(mine, 0, 1)), *riders)

    def core_sum(mine, other, weight, dims):
        came = hop(dot(other, weight, dims, HALF), 0, 1)
        (made,) = tie(dot(mine, weight, dims, HALF))
        made = (made.astype(F32) + came.astype(F32)).astype(HALF)
        return made.reshape(ranks // 2, own, D)

    def group_sum(made, *riders):
        parts = [hop(made[k + 1], *bits) for k, bits in enumerate(near_peers)]
        parts, riders = tie(parts, riders)
        return (sum((part.astype(F32) for part in parts), made[0].astype(F32)), *riders)

    def index_of(shift):
        pairs = []
        for i in range(blocks):
            g = (i // 4) * 2 + i % 2
            far = g + shift
            if 0 <= far < groups and far // per_clip == g // per_clip:
                pairs.append((i, (far // 2) * 4 + (i & PAIR) + far % 2))
        return pairs

    def sided(weight):
        return weight.astype(HALF).reshape(rows, 2, -1)

    qkv_local = inward.astype(HALF).reshape(3, rows, 2, -1).transpose(1, 2, 0, 3)
    local_first = jnp.concatenate(
        [qkv_local.reshape(rows, 2, -1), sided(outward.astype(HALF).T)], axis=-1
    )
    local = [
        None,
        sided(expand),
        sided(contract.astype(HALF).T),
        sided(readout),
    ]

    def sides_of(halves):
        return tuple(
            lax.dynamic_index_in_dim(halves, at, 1, keepdims=False) for at in (side, 1 - side)
        )

    def paired(keep, send):
        came = flip(send, PAIR)
        return jnp.where(side == 0, jnp.stack([keep, came]), jnp.stack([came, keep]))

    small = jnp.concatenate(
        [part.astype(F32).reshape(-1) for part in (token_ids, modality, loss_mask, targets, gains)]
    )[None]
    small = jnp.concatenate([small, flip(small, PAIR)])
    local_first, small = tie(local_first, small)
    masks = [0, PAIR]
    for bit in high_bits + [1]:
        small = jnp.concatenate([small, flip(small, bit)])
        masks = masks + [mask | bit for mask in masks]
    order = blk ^ jnp.arange(blocks)
    mine_first = paired(*sides_of(local_first))
    small = small[jnp.array([masks.index(mask) for mask in range(blocks)])[order]]
    cells = clips * span
    ids_all, modality_all, mask_all, targets_all = (
        small[:, k * cells : (k + 1) * cells]
        .astype(jnp.int32)
        .reshape(blocks, clips, span)
        .transpose(1, 0, 2)
        .reshape(clips, length)
        for k in range(4)
    )
    gains_full = small[:, 4 * cells :].reshape(blocks, 3, rows).transpose(1, 0, 2).reshape(3, D)

    def spread_high(mine, at=slice(None)):
        pieces = [mine[at]]
        for bit in high_bits:
            pieces = pieces + [flip(piece, bit) for piece in pieces]
        return tuple(pieces[1:])

    def both_sides(first, second):
        return tuple(jnp.stack(pair) for pair in zip(first, second))

    def spread_low(pieces):
        return tuple(flip(piece, 1) for piece in pieces)

    def assembled(mine, far, near, grant=40):
        pieces = (mine, *far, *near)
        places = [high ^ (k % highs) if side_at == 0 else low ^ (k // highs)
                  for k in range(len(pieces)) for side_at in range(2)]
        return assembled_at(jnp.stack(places).astype(jnp.int32), pieces, grant)

    mine = [mine_first, None, None, None]
    far = [None] * 4
    near = [None] * 4

    head_order = ((core ^ jnp.arange(2))[:, None] * ys + (y_at ^ jnp.arange(ys))[None]).reshape(-1)

    def by_device(array):
        split = array.reshape(highs, 2, 2, 2, ys, own).transpose(0, 3, 1, 2, 4, 5)
        split = split.reshape(blocks, 2 * ys, own)[:, head_order]
        return split.reshape(blocks, half)

    image_rows = image_table.shape[0]
    code_local = code_table.shape[0]
    table = jnp.concatenate([image_table.astype(HALF), code_table.astype(HALF)])
    ids_dev, modality_dev = by_device(ids_all)[order], by_device(modality_all)[order]
    code_rows = jnp.clip(jnp.where(modality_dev == 1, ids_dev, VT + ids_dev), 0, VT + VA - 1)
    image_at = ids_dev - blk * image_rows
    code_at = code_rows - blk * code_local
    image_at = jnp.where((image_at >= 0) & (image_at < image_rows), image_at, -1)
    code_at = jnp.where((code_at >= 0) & (code_at < code_local), code_at + image_rows, -1)
    table_at = jnp.where(modality_dev == 0, image_at, code_at)
    table_rows = image_rows + code_local
    pick = (table_at.reshape(-1)[:, None] == jnp.arange(table_rows)[None, :]).astype(HALF)
    picked = dot(pick, table, ((1,), (0,)), HALF)
    width = table.shape[1]
    levels = len(all_bits)
    picked = picked.reshape((2,) * levels + (half, width))

    def token_hop(part, bit, left):
        axis = left.index(bit)
        keep = lax.index_in_dim(part, 0, axis, keepdims=False)
        send = lax.index_in_dim(part, 1, axis, keepdims=False)
        return keep + flip(send, bit)

    left = sorted(all_bits, reverse=True)
    mid = width // 2
    picked, mine[0] = tie(picked, mine[0])
    far[0] = spread_high(mine[0])
    part_a = token_hop(picked[..., :mid], 1, left)
    part_b = token_hop(picked[..., mid:], PAIR, left)
    part_a = token_hop(part_a, PAIR, left[:-1])
    part_b = token_hop(part_b, 1, left[:-2] + left[-1:])
    part_a, part_b, mine[0], far[0], local[1:] = tie(part_a, part_b, mine[0], far[0], local[1:])
    local[2:] = [sides_of(halves) for halves in local[2:]]
    mine[1] = paired(*sides_of(local[1]))
    near_own = spread_low(mine[:1])
    for k, bit in enumerate(high_bits[::-1]):
        part_a = token_hop(part_a, bit, left[k:-2])
        part_b = token_hop(part_b, bit, left[k:-2])
    block = jnp.concatenate([part_a, part_b], axis=-1)
    block, mine[1], far[0], near_own, local[2:] = tie(block, mine[1], far[0], near_own, local[2:])
    far_side, near_far = spread_high(mine[1], 0), spread_low(far[0])
    of_core = [
        [block if not bits else hop(block, *bits) for bits in row]
        for row in ([()] + near_peers[: ys - 1], near_peers[ys - 1 :])
    ]
    of_core, far_side, near_far, mine[1], local[2] = tie(
        of_core, far_side, near_far, mine[1], local[2]
    )
    near[0] = (*near_own, *near_far)
    far_other, near_own = spread_high(mine[1], 1), spread_low(mine[1:2])
    mine[2] = paired(*local[2])
    column_pieces = [[row, [hop(piece, 0, 1) for piece in row]] for row in of_core]
    column_at = jnp.stack([head ^ (2 * y + c) for c in range(2) for y in range(ys)])
    normed_in, embedded_own = joined_norm(column_pieces, column_at, gains_full[0], own)
    w_first = assembled(mine[0], far[0], near[0], 60)
    head_columns = w_first.shape[-1] // 4
    w_in, w_out = w_first[:, : 3 * head_columns], w_first[:, 3 * head_columns :]
    local_heads = head_columns // HD
    mixed = dot(normed_in, w_in, ((1,), (0,)), HALF)
    mixed, near_own, far_other, mine[2], local[3] = tie(
        mixed, near_own, far_other, mine[2], local[3]
    )
    mine[3] = paired(*local[3])
    far[1] = both_sides(far_side, far_other)
    far_side = spread_high(mine[2], 0)
    block_order = (
        ((core ^ jnp.arange(2))[:, None, None] * 2 + (side ^ jnp.arange(2))[None, :, None]) * ys
        + (y_at ^ jnp.arange(ys))[None, None]
    ).reshape(-1)
    query_pos = place * team + (block_order[:, None] * own + jnp.arange(own)[None]).reshape(-1)
    query_pos = query_pos.astype(jnp.int32)

    def key_pos(back):
        return jnp.where(query_pos >= back * team, query_pos - back * team, length)

    pairs_own = mixed[:, head_columns:]
    earlier = [lax.ppermute(pairs_own, "blk", index_of(back)) for back in range(1, per_clip)]
    running = attend(
        mixed, mixed, local_heads, query_pos, query_pos, (), per_clip == 1, local_heads
    )
    running, earlier, far_side, far[1], mine[2], mine[3] = tie(
        running, earlier, far_side, far[1], mine[2], mine[3]
    )
    far_other, near_far = spread_high(mine[2], 1), spread_low(far[1])
    for back in range(1, per_clip):
        running = attend(
            mixed,
            earlier[back - 1],
            0,
            query_pos,
            key_pos(back),
            running,
            back == per_clip - 1,
            local_heads,
        )
    flat_heads, log_total = running
    made = core_sum(flat_heads[:half], flat_heads[half:], w_out, ((1,), (1,)))
    made, mine[2] = tie(made, mine[2])
    near_next = spread_low(mine[2:3])
    first, near_far, far_other = group_sum(made, near_far, far_other)
    near[1] = (*near_own, *near_far)
    w_up = assembled(mine[1], far[1], near[1])
    first = embedded_own + first
    far[2] = both_sides(far_side, far_other)
    far_side, near_far = spread_high(mine[3], 0), spread_low(far[2])
    normed_mid, far_side, near_far, near_next, w_up, mine[3] = gathered(
        rms_norm(first, gains_full[1]).astype(HALF), far_side, near_far, near_next, w_up, mine[3]
    )
    near[2] = (*near_next, *near_far)
    w_down = assembled(mine[2], far[2], near[2])
    hidden_up = [dot(part, w_up, ((1,), (0,))) for part in normed_mid]
    active = [jax.nn.gelu(part).astype(HALF) for part in hidden_up]
    near_own, far_other = spread_low(mine[3:]), spread_high(mine[3], 1)
    made = core_sum(*active, w_down, ((1,), (1,)))
    second, near_own, far_other = group_sum(made, near_own, far_other)
    far[3] = both_sides(far_side, far_other)
    second = first + second
    final_in, *near_far = gathered(
        rms_norm(second, gains_full[2]).astype(HALF), *spread_low(far[3])
    )
    w_read = assembled(mine[3], far[3], (*near_own, *near_far))
    logits = [dot(part, w_read, ((1,), (0,))) for part in final_in]

    def of_team(array):
        taken = lax.dynamic_slice(array, (clip, place * team), (1, team))
        return taken.reshape(ranks, own)[block_order].reshape(team)

    weight_all = (
        (mask_all == 1) & (jnp.arange(length)[None, :] < clip_lengths[:, None])
    ).astype(F32)
    loss_count = jnp.sum(weight_all)
    weight_of = of_team(weight_all)
    targets_own = of_team(targets_all)
    vocab_local = logits[0].shape[1]
    column_ids = (head * 2 + side) * vocab_local + jnp.arange(vocab_local)
    halves = (slice(0, half), slice(half, team))
    match = [column_ids[None, :] == targets_own[at][:, None] for at in halves]
    parts = []
    for part, hit in zip(logits, match):
        top = jnp.max(part, axis=-1)
        total = jnp.sum(jnp.exp(part - top[:, None]), axis=-1)
        parts.append(jnp.stack([top, total, jnp.sum(jnp.where(hit, part, 0.0), axis=-1)]))
    stats = jnp.concatenate(parts, axis=1)
    for axis, bits in [(2, (PAIR, 0)), (1, (0, 1))] + [
        (3, (0, 2 << k)) for k in range(ys.bit_length() - 1)
    ]:
        other = hop(stats, *bits).reshape(3, 2, 2, ys, own)
        flipped = np.arange(other.shape[axis]) ^ (bits[1] // 2 if axis == 3 else 1)
        other = jnp.stack(
            [lax.index_in_dim(other, k, axis, keepdims=False) for k in flipped], axis=axis
        ).reshape(3, team)
        top = jnp.maximum(stats[0], other[0])
        total = stats[1] * jnp.exp(stats[0] - top) + other[1] * jnp.exp(other[0] - top)
        stats = jnp.stack([top, total, stats[2] + other[2]])
    log_norm = stats[0] + jnp.log(stats[1])
    per_token = (log_norm + ZCOEF * log_norm * log_norm - stats[2]) * weight_of
    loss_part = jnp.sum(per_token) * (rank == 0).astype(F32)

    token_grad = weight_of / loss_count
    grad_logits = []
    for part, hit, at in zip(logits, match, halves):
        probs = jnp.exp(part - log_norm[at][:, None])
        scaled = probs * (1.0 + 2.0 * ZCOEF * log_norm[at])[:, None] - hit.astype(F32)
        grad_logits.append((token_grad[at][:, None] * scaled).astype(HALF))

    top_bit = high_bits[-1]
    top = (blk // top_bit) % 2

    def made_of(left, right):
        return dot(left, right, ((0,), (0,)), HALF).reshape(
            2, highs // 2, 2, 2, rows, right.shape[1]
        )

    def low_part(made, at_top, at_low):
        chosen = lax.dynamic_index_in_dim(made, at_top, 0, keepdims=False)
        return lax.dynamic_index_in_dim(chosen, at_low, 2, keepdims=False)

    def send_low(made, at_top):
        return flip(low_part(made, at_top, 1 - low), 1)

    def add_low(made, at_top, came):
        return low_part(made, at_top, low).astype(F32) + came.astype(F32)

    def for_top(made, came):
        total = add_low(made, 1 - top, came).astype(HALF)
        return total[:, 0], total[:, 1]

    def send_high(part):
        return flip(part, top_bit)

    def add_high(made, came_low, came_high):
        total = add_low(made, top, came_low) + jnp.stack(came_high, axis=1).astype(F32)
        total = total.reshape((2,) * (len(high_bits) - 1) + total.shape[1:])
        for bit in high_bits[-2::-1] if len(high_bits) > 1 else []:
            at = (blk // bit) % 2
            send = lax.dynamic_index_in_dim(total, 1 - at, 0, keepdims=False)
            keep = lax.dynamic_index_in_dim(total, at, 0, keepdims=False)
            total = keep + flip(send.astype(HALF), bit).astype(F32)
        return total

    def sum_sides(total):
        send = lax.dynamic_index_in_dim(total, 1 - side, 0, keepdims=False)
        keep = lax.dynamic_index_in_dim(total, side, 0, keepdims=False)
        came = flip(send.astype(HALF), PAIR).astype(F32)
        return jnp.where(side == 0, keep, came), jnp.where(side == 0, came, keep)

    def joined(parts):
        return jnp.concatenate(parts)

    made = core_sum(*grad_logits, w_read, ((1,), (1,)))
    made, read_made = tie(made, made_of(joined(final_in), joined(grad_logits)))
    read_far = send_low(read_made, 1 - top)
    grad_final, read_made, read_far = group_sum(made, read_made, read_far)
    read_near = send_low(read_made, top)
    read_top = for_top(read_made, read_far)
    read_first = send_high(read_top[0])
    grad_second, gain_final = norm_back(second, gains_full[2], grad_final)
    branch_grad, read_near, read_first, read_top = gathered(
        grad_second.astype(HALF), read_near, read_first, read_top
    )
    read_second = send_high(read_top[1])
    grad_hidden = []
    for part, up in zip(branch_grad, hidden_up):
        unused_gelu, gelu_pull = jax.vjp(jax.nn.gelu, up)
        grad_hidden.append(gelu_pull(dot(part, w_down, ((1,), (0,))))[0].astype(HALF))
    made = core_sum(*grad_hidden, w_up, ((1,), (1,)))
    made, normed_mid, grad_hidden, read_second, down_made = tie(
        made,
        normed_mid,
        grad_hidden,
        read_second,
        made_of(joined(branch_grad), joined(active)),
    )
    read_total = add_high(read_made, read_near, (read_first, read_second))
    down_far = send_low(down_made, 1 - top)
    grad_mid, down_made, down_far, up_made = group_sum(
        made, down_made, down_far, made_of(joined(normed_mid), joined(grad_hidden))
    )
    down_near = send_low(down_made, top)
    down_top = for_top(down_made, down_far)
    down_first = send_high(down_top[0])
    grad_mid_in, gain_mid = norm_back(first, gains_full[1], grad_mid)
    grad_first = grad_second + grad_mid_in
    attn_grad, up_made, down_near, down_first, down_top, read_total = gathered(
        grad_first.astype(HALF), up_made, down_near, down_first, down_top, read_total
    )
    down_second = send_high(down_top[1])
    up_far = send_low(up_made, 1 - top)
    attn_grad = joined(attn_grad)
    grad_heads = dot(attn_grad, w_out, ((1,), (0,)), HALF)
    returned = []
    grad_query = None
    for back in range(1, per_clip):
        grad_query, far_pairs = attend_back(
            mixed,
            earlier[back - 1],
            0,
            query_pos,
            key_pos(back),
            flat_heads,
            grad_heads,
            log_total,
            grad_query,
            False,
            local_heads,
        )
        if back == 1:
            far_pairs, up_made, up_far, down_second, read_total = tie(
                far_pairs, up_made, up_far, down_second, read_total
            )
            grad_read = sum_sides(read_total)
            grad_down = sum_sides(add_high(down_made, down_near, (down_first, down_second)))
            up_near = send_low(up_made, top)
            up_top = for_top(up_made, up_far)
            up_first = send_high(up_top[0])
        returned.append(lax.ppermute(far_pairs, "blk", index_of(-back)))
    grad_query, grad_pairs = attend_back(
        mixed,
        mixed,
        local_heads,
        query_pos,
        query_pos,
        flat_heads,
        grad_heads,
        log_total,
        grad_query,
        True,
        local_heads,
    )
    for far_pairs in returned:
        grad_pairs = grad_pairs + far_pairs.astype(F32)
    grad_mixed = jnp.concatenate([grad_query, grad_pairs.astype(HALF)], axis=1)
    grad_mixed, up_first, up_top, grad_read = tie(grad_mixed, up_first, up_top, grad_read)
    up_second = send_high(up_top[1])
    made = core_sum(grad_mixed[:half], grad_mixed[half:], w_in, ((1,), (1,)))
    made, in_made, out_made, up_near, grad_down = tie(
        made,
        made_of(normed_in, grad_mixed),
        made_of(attn_grad, flat_heads),
        up_near,
        grad_down,
    )
    in_far, out_far = send_low(in_made, 1 - top), send_low(out_made, 1 - top)
    grad_norm_in, in_made, out_made, in_far, out_far, up_second = group_sum(
        made, in_made, out_made, in_far, out_far, up_second
    )
    in_near, out_near = send_low(in_made, top), send_low(out_made, top)
    in_top, out_top = for_top(in_made, in_far), for_top(out_made, out_far)
    in_first, out_first = send_high(in_top[0]), send_high(out_top[0])
    grad_embed_in, gain_in = norm_back(embedded_own, gains_full[0], grad_norm_in)
    grad_embed = (grad_first + grad_embed_in).astype(HALF)

    def columns_of(head_bits):
        at = (head ^ head_bits) * width
        return lax.dynamic_slice(grad_embed, (0, at), (own, width))

    head_bits = [2 * y + c for c in range(2) for y in range(ys)]
    head_parts = [
        columns_of(bits) if bits == 0 else hop(columns_of(bits), 0, bits) for bits in head_bits
    ]
    grad_up = sum_sides(add_high(up_made, up_near, (up_first, up_second)))
    columns_own = jnp.concatenate(head_parts)
    gain_own = jnp.stack([gain_in, gain_mid, gain_final])
    for k in range(heads.bit_length() - 1):
        gain_own = gain_own + hop(gain_own, 0, 1 << k)

    def spread(pieces, bit):
        return jnp.concatenate([pieces, flip(pieces, bit)])

    mid = width // 2
    gain_rows = gain_own.astype(HALF).reshape(-1, width - mid)
    gain_rows = jnp.pad(gain_rows, ((0, -gain_rows.shape[0] % 16), (0, 0)))
    pieces_a, pieces_b = tie(
        columns_own[None, :, :mid], jnp.concatenate([columns_own[:, mid:], gain_rows])[None]
    )
    for bit in high_bits[::-1]:
        pieces_a, pieces_b = spread(pieces_a, bit), spread(pieces_b, bit)
    pieces_a, pieces_b, in_first, out_first, in_top, out_top, in_near, out_near = tie(
        pieces_a, pieces_b, in_first, out_first, in_top, out_top, in_near, out_near
    )
    in_second, out_second = send_high(in_top[1]), send_high(out_top[1])
    pieces_a, pieces_b = spread(pieces_a, PAIR), spread(pieces_b, 1)
    pieces_a, pieces_b, in_second, out_second, grad_up = tie(
        pieces_a, pieces_b, in_second, out_second, grad_up
    )
    pieces = (pieces_a, flip(pieces_a, 1), pieces_b, flip(pieces_b, PAIR))
    pieces, in_total, out_total = tie(
        pieces,
        add_high(in_made, in_near, (in_first, in_second)),
        add_high(out_made, out_near, (out_first, out_second)),
    )
    grad_in, grad_out_w = sum_sides(in_total), sum_sides(out_total)
    gain_sum = sum(jnp.sum(part[:, half:].astype(F32), axis=0) for part in pieces[2:])
    gain_sum = gain_sum.reshape(-1)[: 3 * D].reshape(3, D)
    gain_sum = lax.dynamic_slice_in_dim(gain_sum, blk * rows, rows, 1)
    masks_a, masks_b = [0], [0]
    for bit_a, bit_b in zip(high_bits[::-1] + [PAIR, 1], high_bits[::-1] + [1, PAIR]):
        masks_a = masks_a + [mask | bit_a for mask in masks_a]
        masks_b = masks_b + [mask | bit_b for mask in masks_b]
    places = [[masks.index(mask) for mask in range(blocks)] for masks in (masks_a, masks_b)]
    row_step = max(s for s in range(8, 321, 8) if table_rows % s == 0)
    grad_table = table_grad(table_at, pieces, places, table_rows, row_step)
    img_sum, code_sum = grad_table[:image_rows], grad_table[image_rows:]

    in_sum = jnp.stack(
        [
            jnp.concatenate(
                [part[:, k * head_columns : (k + 1) * head_columns] for part in grad_in], axis=1
            )
            for k in range(3)
        ]
    )
    out_sum = jnp.concatenate([part.T for part in grad_out_w])
    down_sum = jnp.concatenate([part.T for part in grad_down])
    up_sum = jnp.concatenate(grad_up, axis=1)
    read_sum = jnp.concatenate(grad_read, axis=1)
    in_sum, out_sum, up_sum, down_sum, read_sum = (
        with_layout_constraint(total, Layout(major_to_minor=tuple(range(total.ndim))))
        for total in (in_sum, out_sum, up_sum, down_sum, read_sum)
    )
    sums = [in_sum, out_sum, up_sum, down_sum, img_sum, code_sum, read_sum, gain_sum]
    local_squares = jnp.float32(0.0)
    for shard in sums[:7]:
        local_squares = local_squares + jnp.sum(shard * shard)
    local_squares = local_squares + (head == 0).astype(F32) * jnp.sum(gain_sum * gain_sum)
    mine = jnp.broadcast_to(
        jnp.stack([local_squares, loss_part])[None, :, None], (blocks * heads, 2, 128)
    )
    totals = jnp.sum(lax.all_to_all(mine, both, 0, 0, tiled=True), axis=0)
    grad_norm = jnp.sqrt(totals[0, 0])
    loss_sum = totals[1, 0]
    factor = jnp.minimum(1.0, CLIP / grad_norm)
    spreads = [
        D ** (-0.5),
        (length // 2) ** 0.5 * D ** (-0.5),
        D ** (-0.5),
        FF ** (-0.5),
        0.05,
        0.05,
        2.0 * D ** (-0.5),
    ]
    weights = [inward, outward, expand, contract, image_table, code_table, readout, gains]
    firsts = [
        inward_first,
        outward_first,
        expand_first,
        contract_first,
        image_first,
        code_first,
        readout_first,
        gains_first,
    ]
    seconds = [
        inward_second,
        outward_second,
        expand_second,
        contract_second,
        image_second,
        code_second,
        readout_second,
        gains_second,
    ]
    result = []
    for index in range(8):
        rate = GAIN_RATE if index == 7 else RATE_FACTOR * spreads[index]
        decay = 0.0 if index == 7 else DECAY
        result.extend(
            adamw(weights[index], firsts[index], seconds[index], sums[index] * factor, rate, decay)
        )
    return (*result, loss_sum, loss_count, grad_norm)


def solution(mesh):
    matrices = (
        P(None, "blk", "head"),
        P("head", "blk"),
        P("blk", "head"),
        P("head", "blk"),
        P("blk", "head"),
        P("blk", "head"),
        P("blk", "head"),
        P(None, "blk"),
    )
    tokens = P(None, "blk")
    return jax.shard_map(
        shards,
        mesh=mesh,
        in_specs=matrices * 3 + (tokens, tokens, P(), tokens, tokens),
        out_specs=tuple(spec for spec in matrices for _ in range(3)) + (P(), P(), P()),
        check_vma=False,
    )
```

```python
import jax
import jax.numpy as jnp
import numpy as np
from jax import lax
from jax.experimental import pallas as pl
from jax.experimental.layout import Layout, with_layout_constraint
from jax.experimental.pallas import tpu as pltpu
from jax.sharding import PartitionSpec as P

D = 2048
HD = 128
FF = 8192
VT = 1024
VA = 256
STEP = 10


EPS = 1e-05
ZCOEF = 0.01
CLIP = 0.02
BETA1 = 0.9
BETA2 = 0.95
ADAM_EPS = 1e-08
DECAY = 0.1
RATE_FACTOR = 1.5
GAIN_RATE = 0.8

HALF = jnp.bfloat16
F32 = jnp.float32
NEG = -1e30
LOG2E = 1.4426950408889634
SCORE = HD ** (-0.5) * LOG2E
PAIR = 2


def flip(value, bit):
    count = lax.axis_size("blk")
    return lax.ppermute(value, "blk", [(i, i ^ bit) for i in range(count)])


def rms_norm(hidden, gain):
    return hidden * lax.rsqrt(jnp.mean(hidden * hidden, axis=-1, keepdims=True) + EPS) * gain


def norm_back(hidden, gain, upstream):
    unused, pullback = jax.vjp(rms_norm, hidden, gain)
    return pullback(upstream)


def dot(left, right, dims, out=F32):
    return lax.dot_general(left, right, (dims, ((), ())), preferred_element_type=F32).astype(out)


def adamw(weight, first, second, grad, rate, decay):
    first = BETA1 * first + (1.0 - BETA1) * grad
    second = BETA2 * second + (1.0 - BETA2) * grad * grad
    first_hat = first / (1.0 - BETA1**STEP)
    second_hat = second / (1.0 - BETA2**STEP)
    weight = weight - rate * (first_hat / (jnp.sqrt(second_hat) + ADAM_EPS) + decay * weight)
    return (weight, first, second)


def dot_last(left, right):
    return lax.dot_general(left, right, (((1,), (1,)), ((), ())), preferred_element_type=F32)


def dot_first(left, right):
    return lax.dot_general(left, right, (((0,), (0,)), ((), ())), preferred_element_type=F32)


def attend_kernel(opening, closing, qpos_ref, kpos_ref, q_ref, k_ref, v_ref, *refs):
    scores = dot_last(k_ref[...], q_ref[...]) * SCORE
    scores = jnp.where(kpos_ref[...] <= qpos_ref[...], scores, NEG)
    top = jnp.max(scores, axis=0, keepdims=True)
    if not opening:
        acc_in, top_in, total_in = refs[:3]
        refs = refs[3:]
        top = jnp.maximum(top, top_in[0])
    weights = jnp.exp2(scores - top)
    total = jnp.sum(weights, axis=0, keepdims=True)
    acc = dot_first(v_ref[...], weights.astype(HALF))
    if not opening:
        fading = jnp.exp2(top_in[0] - top)
        total = total + total_in[0] * fading
        acc = acc + acc_in[0] * fading
    if closing:
        out_ref, log_ref = refs
        out_ref[...] = (acc / total).T.astype(HALF)
        log_ref[0] = top + jnp.log2(total)
    else:
        acc_ref, top_ref, total_ref = refs
        acc_ref[0] = acc
        top_ref[0] = top
        total_ref[0] = total


def attend(queries, pairs, at, query_pos, key_pos, state, closing, count):
    team = queries.shape[0]
    step = min(team, 256)
    row = pl.BlockSpec((1, 1, step), lambda h, i: (h, 0, i))
    wide = pl.BlockSpec((1, HD, step), lambda h, i: (h, 0, i))
    rows = jax.ShapeDtypeStruct((count, 1, team), F32)
    if closing:
        out_specs = [pl.BlockSpec((step, HD), lambda h, i: (i, h)), row]
        out_shape = [jax.ShapeDtypeStruct((team, count * HD), HALF), rows]
    else:
        out_specs = [wide, row, row]
        out_shape = [jax.ShapeDtypeStruct((count, HD, team), F32), rows, rows]
    return pl.pallas_call(
        lambda *refs: attend_kernel(not state, closing, *refs),
        grid=(count, team // step),
        in_specs=[
            pl.BlockSpec((1, step), lambda h, i: (0, i)),
            pl.BlockSpec((team, 1), lambda h, i: (0, 0)),
            pl.BlockSpec((step, HD), lambda h, i: (i, h)),
            pl.BlockSpec((team, HD), lambda h, i: (0, at + h)),
            pl.BlockSpec((team, HD), lambda h, i: (0, at + count + h)),
        ]
        + ([wide, row, row] if state else []),
        out_specs=out_specs,
        out_shape=out_shape,
        compiler_params=pltpu.CompilerParams(vmem_limit_bytes=40 * 2**20),
        cost_estimate=pl.CostEstimate(
            flops=4 * count * team * team * HD,
            bytes_accessed=10 * count * team * HD,
            transcendentals=count * team * team,
        ),
    )(query_pos[None], key_pos[:, None], queries, pairs, pairs, *state)


def attend_back_kernel(opening, closing, qpos_ref, kpos_ref, q_ref, k_ref, v_ref, *refs):
    out_ref, grad_ref, log_ref = refs[:3]
    query_in, (query_ref, pair_ref, keys_acc, values_acc) = refs[3:-4], refs[-4:]
    head, step = pl.program_id(0), pl.program_id(1)
    grad = grad_ref[...]
    inner = (grad.astype(F32) * out_ref[...].astype(F32)).T
    inner = jnp.sum(inner, axis=0, keepdims=True)
    scores = dot_last(k_ref[...], q_ref[...]) * SCORE
    seen = kpos_ref[...] <= qpos_ref[...]
    probs = jnp.where(seen, jnp.exp2(scores - log_ref[0]), 0.0)
    grad_probs = dot_last(v_ref[...], grad)
    grad_scores = (probs * (grad_probs - inner)).astype(HALF)
    grad_query = dot_first(k_ref[...], grad_scores)
    if not opening:
        grad_query = grad_query + query_in[0][0]
    if closing:
        query_ref[...] = (grad_query * HD ** (-0.5)).T.astype(HALF)
    else:
        query_ref[0] = grad_query

    @pl.when(step == 0)
    def clear():
        keys_acc[...] = jnp.zeros_like(keys_acc)
        values_acc[...] = jnp.zeros_like(values_acc)

    keys_acc[...] += jnp.dot(grad_scores, q_ref[...], preferred_element_type=F32)
    values_acc[...] += jnp.dot(probs.astype(HALF), grad, preferred_element_type=F32)

    @pl.when(step == pl.num_programs(1) - 1)
    def write():
        half = pair_ref.shape[1] // 2
        at = pl.multiple_of(head * HD, HD)
        pair_ref[:, pl.ds(at, HD)] = (keys_acc[...] * HD ** (-0.5)).astype(pair_ref.dtype)
        pair_ref[:, pl.ds(half + at, HD)] = values_acc[...].astype(pair_ref.dtype)


def attend_back(queries, pairs, at, query_pos, key_pos, out, grad, log_total, state, closing, count):
    team = queries.shape[0]
    step = min(team, 256)
    wide = pl.BlockSpec((1, HD, step), lambda h, i: (h, 0, i))
    block = pl.BlockSpec((step, HD), lambda h, i: (i, h))
    if closing:
        query_spec, query_shape = block, jax.ShapeDtypeStruct((team, count * HD), HALF)
    else:
        query_spec, query_shape = wide, jax.ShapeDtypeStruct((count, HD, team), F32)
    return pl.pallas_call(
        lambda *refs: attend_back_kernel(state is None, closing, *refs),
        grid=(count, team // step),
        in_specs=[
            pl.BlockSpec((1, step), lambda h, i: (0, i)),
            pl.BlockSpec((team, 1), lambda h, i: (0, 0)),
            block,
            pl.BlockSpec((team, HD), lambda h, i: (0, at + h)),
            pl.BlockSpec((team, HD), lambda h, i: (0, at + count + h)),
            block,
            block,
            pl.BlockSpec((1, 1, step), lambda h, i: (h, 0, i)),
        ]
        + ([] if state is None else [wide]),
        out_specs=[query_spec, pl.BlockSpec((team, 2 * count * HD), lambda h, i: (0, 0))],
        out_shape=[
            query_shape,
            jax.ShapeDtypeStruct((team, 2 * count * HD), F32 if closing else HALF),
        ],
        scratch_shapes=[pltpu.VMEM((team, HD), F32), pltpu.VMEM((team, HD), F32)],
        compiler_params=pltpu.CompilerParams(vmem_limit_bytes=48 * 2**20),
        cost_estimate=pl.CostEstimate(
            flops=10 * count * team * team * HD,
            bytes_accessed=20 * count * team * HD,
            transcendentals=count * team * team,
        ),
    )(
        query_pos[None],
        key_pos[:, None],
        queries,
        pairs,
        pairs,
        out,
        grad,
        log_total,
        *([] if state is None else [state]),
    )


def joined_norm_kernel(sides, at_ref, gain_ref, *refs):
    pieces, out_ref, first_ref = refs[:-2], refs[-2], refs[-1]
    count = len(pieces) // sides
    width = pieces[0].shape[1]
    is_first = (pl.program_id(0) == 0) & (pl.program_id(1) == 0)
    for side in range(sides):
        parts = [ref[...].astype(F32) for ref in pieces[side * count : (side + 1) * count]]
        squares = sum(jnp.sum(part * part, axis=-1, keepdims=True) for part in parts)
        scale = lax.rsqrt(squares / (count * width) + EPS)
        for k, part in enumerate(parts):
            at = pl.ds(pl.multiple_of(at_ref[k] * width, width), width)
            out_ref[0, side, 0, :, at] = (part * scale * gain_ref[:, at]).astype(HALF)
            if side == 0:

                @pl.when(is_first)
                def keep():
                    first_ref[:, at] = part


def joined_norm(pieces, at, gain, own):
    ys = len(pieces[0][0])
    width = pieces[0][0][0].shape[1]
    columns = 2 * ys * width
    flat, specs = [], []
    for of_side in pieces:
        for core, of_core in enumerate(of_side):
            for y, piece in enumerate(of_core):
                flat.append(piece)
                specs.append(
                    pl.BlockSpec(
                        (own, width),
                        lambda c, k, at, core=core, y=y: ((c ^ core) * ys + (k ^ y), 0),
                    )
                )
    grid = pltpu.PrefetchScalarGridSpec(
        num_scalar_prefetch=1,
        grid=(2, ys),
        in_specs=[pl.BlockSpec((1, columns), lambda c, k, at: (0, 0))] + specs,
        out_specs=[
            pl.BlockSpec((1, 2, 1, own, columns), lambda c, k, at: (c, 0, k, 0, 0)),
            pl.BlockSpec((own, columns), lambda c, k, at: (0, 0)),
        ],
    )
    normed, first = pl.pallas_call(
        lambda *refs: joined_norm_kernel(2, *refs),
        grid_spec=grid,
        out_shape=[
            jax.ShapeDtypeStruct((2, 2, ys, own, columns), HALF),
            jax.ShapeDtypeStruct((own, columns), F32),
        ],
        compiler_params=pltpu.CompilerParams(vmem_limit_bytes=60 * 2**20),
        cost_estimate=pl.CostEstimate(
            flops=20 * ys * own * columns, bytes_accessed=16 * ys * own * columns, transcendentals=0
        ),
    )(at, gain[None], *flat)
    return normed.reshape(4 * ys * own, columns), first


def table_grad_kernel(places, at_ref, *refs):
    parts, out_ref = refs[:-1], refs[-1]
    tokens = at_ref.shape[1]
    width = parts[0].shape[2]
    step = out_ref.shape[0]
    row = pl.program_id(0) * step + lax.broadcasted_iota(jnp.int32, (step, tokens), 0)
    for part, order in enumerate(places):
        total = jnp.zeros((step, width), F32)
        for k, place in enumerate(order):
            pieces, at = parts[2 * part + place // (len(order) // 2)], place % (len(order) // 2)
            pick = (row == at_ref[k][None, :]).astype(F32).astype(HALF)
            total += jnp.dot(pick, pieces[at, :tokens], preferred_element_type=F32)
        out_ref[:, part * width : (part + 1) * width] = total


def table_grad(at, parts, places, rows, step):
    count, tokens = at.shape
    columns = parts[0].shape[2] * len(places)
    return pl.pallas_call(
        lambda *refs: table_grad_kernel(places, *refs),
        grid=(rows // step,),
        in_specs=[pl.BlockSpec((count, tokens), lambda i: (0, 0))]
        + [pl.BlockSpec(part.shape, lambda i: (0, 0, 0)) for part in parts],
        out_specs=pl.BlockSpec((step, columns), lambda i: (i, 0)),
        out_shape=jax.ShapeDtypeStruct((rows, columns), F32),
        compiler_params=pltpu.CompilerParams(vmem_limit_bytes=56 * 2**20),
        cost_estimate=pl.CostEstimate(
            flops=2 * rows * count * tokens * columns,
            bytes_accessed=2 * count * tokens * columns + 4 * rows * columns,
            transcendentals=0,
        ),
    )(at, *parts)


def assembled_kernel(count, at_ref, *refs):
    pieces, out_ref = refs[:count], refs[count]
    for k, piece in enumerate(pieces):

        @pl.when(pl.program_id(0) == k)
        def write():
            out_ref[0, :, 0] = piece[...]


def assembled_at(places, pieces, grant):
    count = len(pieces)
    unused, rows, columns = pieces[0].shape
    grid = pltpu.PrefetchScalarGridSpec(
        num_scalar_prefetch=1,
        grid=(count,),
        in_specs=[pl.BlockSpec((2, rows, columns), lambda i, at: (0, 0, 0)) for piece in pieces],
        out_specs=pl.BlockSpec(
            (1, 2, 1, rows, columns), lambda i, at: (at[2 * i], 0, at[2 * i + 1], 0, 0)
        ),
    )
    whole = pl.pallas_call(
        lambda *refs: assembled_kernel(count, *refs),
        grid_spec=grid,
        out_shape=jax.ShapeDtypeStruct((count // 2, 2, 2, rows, columns), HALF),
        compiler_params=pltpu.CompilerParams(vmem_limit_bytes=grant * 2**20),
        cost_estimate=pl.CostEstimate(
            flops=0, bytes_accessed=4 * count * pieces[0].size, transcendentals=0
        ),
    )(places, *pieces)
    return whole.reshape(count * 2 * rows, columns)


def shards(
    inward,
    outward,
    expand,
    contract,
    image_table,
    code_table,
    readout,
    gains,
    inward_first,
    outward_first,
    expand_first,
    contract_first,
    image_first,
    code_first,
    readout_first,
    gains_first,
    inward_second,
    outward_second,
    expand_second,
    contract_second,
    image_second,
    code_second,
    readout_second,
    gains_second,
    token_ids,
    modality,
    clip_lengths,
    loss_mask,
    targets,
):
    blocks = lax.axis_size("blk")
    heads = lax.axis_size("head")
    blk = lax.axis_index("blk")
    head = lax.axis_index("head")
    clips, span = token_ids.shape
    length = span * blocks
    rows = D // blocks
    low = blk % 2
    side = (blk // 2) % 2
    high = blk // 4
    highs = blocks // 4
    groups = blocks // 2
    group = high * 2 + low
    per_clip = groups // clips
    clip = group // per_clip
    place = group % per_clip
    ranks = 2 * heads
    core, y_at, ys = head % 2, head // 2, heads // 2
    rank = side * heads + head
    team = clips * length // groups
    half = team // 2
    own = team // ranks
    high_bits = [1 << k for k in range(2, blocks.bit_length() - 1)]
    all_bits = [1, 2] + high_bits
    both = ("blk", "head")
    near_peers = [(side_bit, 2 * y) for side_bit in (0, PAIR) for y in range(ys)][1:]

    def hop(value, blk_bits, head_bits):
        pairs = [
            (i * heads + h, (i ^ blk_bits) * heads + (h ^ head_bits))
            for i in range(blocks)
            for h in range(heads)
        ]
        return lax.ppermute(value, both, pairs)

    def tie(*values):
        return lax.optimization_barrier(values)

    def gathered(block, *riders):
        parts, riders = tie([hop(block, *bits) for bits in near_peers], riders)
        mine = jnp.concatenate([block] + parts)
        return ((mine, hop(mine, 0, 1)), *riders)

    def core_sum(mine, other, weight, dims):
        came = hop(dot(other, weight, dims, HALF), 0, 1)
        (made,) = tie(dot(mine, weight, dims, HALF))
        made = (made.astype(F32) + came.astype(F32)).astype(HALF)
        return made.reshape(ranks // 2, own, D)

    def group_sum(made, *riders):
        parts = [hop(made[k + 1], *bits) for k, bits in enumerate(near_peers)]
        parts, riders = tie(parts, riders)
        return (sum((part.astype(F32) for part in parts), made[0].astype(F32)), *riders)

    def index_of(shift):
        pairs = []
        for i in range(blocks):
            g = (i // 4) * 2 + i % 2
            far = g + shift
            if 0 <= far < groups and far // per_clip == g // per_clip:
                pairs.append((i, (far // 2) * 4 + (i & PAIR) + far % 2))
        return pairs

    def sided(weight):
        return weight.astype(HALF).reshape(rows, 2, -1)

    qkv_local = inward.astype(HALF).reshape(3, rows, 2, -1).transpose(1, 2, 0, 3)
    local_first = jnp.concatenate(
        [qkv_local.reshape(rows, 2, -1), sided(outward.astype(HALF).T)], axis=-1
    )
    local = [
        None,
        sided(expand),
        sided(contract.astype(HALF).T),
        sided(readout),
    ]

    def sides_of(halves):
        return tuple(
            lax.dynamic_index_in_dim(halves, at, 1, keepdims=False) for at in (side, 1 - side)
        )

    def paired(keep, send):
        came = flip(send, PAIR)
        return jnp.where(side == 0, jnp.stack([keep, came]), jnp.stack([came, keep]))

    small = jnp.concatenate(
        [part.astype(F32).reshape(-1) for part in (token_ids, modality, loss_mask, targets, gains)]
    )[None]
    small = jnp.concatenate([small, flip(small, PAIR)])
    local_first, small = tie(local_first, small)
    masks = [0, PAIR]
    for bit in high_bits + [1]:
        small = jnp.concatenate([small, flip(small, bit)])
        masks = masks + [mask | bit for mask in masks]
    order = blk ^ jnp.arange(blocks)
    mine_first = paired(*sides_of(local_first))
    small = small[jnp.array([masks.index(mask) for mask in range(blocks)])[order]]
    cells = clips * span
    ids_all, modality_all, mask_all, targets_all = (
        small[:, k * cells : (k + 1) * cells]
        .astype(jnp.int32)
        .reshape(blocks, clips, span)
        .transpose(1, 0, 2)
        .reshape(clips, length)
        for k in range(4)
    )
    gains_full = small[:, 4 * cells :].reshape(blocks, 3, rows).transpose(1, 0, 2).reshape(3, D)

    def spread_high(mine, at=slice(None)):
        pieces = [mine[at]]
        for bit in high_bits:
            pieces = pieces + [flip(piece, bit) for piece in pieces]
        return tuple(pieces[1:])

    def both_sides(first, second):
        return tuple(jnp.stack(pair) for pair in zip(first, second))

    def spread_low(pieces):
        return tuple(flip(piece, 1) for piece in pieces)

    def assembled(mine, far, near, grant=40):
        pieces = (mine, *far, *near)
        places = [high ^ (k % highs) if side_at == 0 else low ^ (k // highs)
                  for k in range(len(pieces)) for side_at in range(2)]
        return assembled_at(jnp.stack(places).astype(jnp.int32), pieces, grant)

    mine = [mine_first, None, None, None]
    far = [None] * 4
    near = [None] * 4

    head_order = ((core ^ jnp.arange(2))[:, None] * ys + (y_at ^ jnp.arange(ys))[None]).reshape(-1)

    def by_device(array):
        split = array.reshape(highs, 2, 2, 2, ys, own).transpose(0, 3, 1, 2, 4, 5)
        split = split.reshape(blocks, 2 * ys, own)[:, head_order]
        return split.reshape(blocks, half)

    image_rows = image_table.shape[0]
    code_local = code_table.shape[0]
    table = jnp.concatenate([image_table.astype(HALF), code_table.astype(HALF)])
    ids_dev, modality_dev = by_device(ids_all)[order], by_device(modality_all)[order]
    code_rows = jnp.clip(jnp.where(modality_dev == 1, ids_dev, VT + ids_dev), 0, VT + VA - 1)
    image_at = ids_dev - blk * image_rows
    code_at = code_rows - blk * code_local
    image_at = jnp.where((image_at >= 0) & (image_at < image_rows), image_at, -1)
    code_at = jnp.where((code_at >= 0) & (code_at < code_local), code_at + image_rows, -1)
    table_at = jnp.where(modality_dev == 0, image_at, code_at)
    table_rows = image_rows + code_local
    pick = (table_at.reshape(-1)[:, None] == jnp.arange(table_rows)[None, :]).astype(HALF)
    picked = dot(pick, table, ((1,), (0,)), HALF)
    width = table.shape[1]
    levels = len(all_bits)
    picked = picked.reshape((2,) * levels + (half, width))

    def token_hop(part, bit, left):
        axis = left.index(bit)
        keep = lax.index_in_dim(part, 0, axis, keepdims=False)
        send = lax.index_in_dim(part, 1, axis, keepdims=False)
        return keep + flip(send, bit)

    left = sorted(all_bits, reverse=True)
    mid = width // 2
    picked, mine[0] = tie(picked, mine[0])
    far[0] = spread_high(mine[0])
    part_a = token_hop(picked[..., :mid], 1, left)
    part_b = token_hop(picked[..., mid:], PAIR, left)
    part_a = token_hop(part_a, PAIR, left[:-1])
    part_b = token_hop(part_b, 1, left[:-2] + left[-1:])
    part_a, part_b, mine[0], far[0], local[1:] = tie(part_a, part_b, mine[0], far[0], local[1:])
    local[2:] = [sides_of(halves) for halves in local[2:]]
    mine[1] = paired(*sides_of(local[1]))
    near_own = spread_low(mine[:1])
    for k, bit in enumerate(high_bits[::-1]):
        part_a = token_hop(part_a, bit, left[k:-2])
        part_b = token_hop(part_b, bit, left[k:-2])
    block = jnp.concatenate([part_a, part_b], axis=-1)
    block, mine[1], far[0], near_own, local[2:] = tie(block, mine[1], far[0], near_own, local[2:])
    far_side, near_far = spread_high(mine[1], 0), spread_low(far[0])
    of_core = [
        [block if not bits else hop(block, *bits) for bits in row]
        for row in ([()] + near_peers[: ys - 1], near_peers[ys - 1 :])
    ]
    of_core, far_side, near_far, mine[1], local[2] = tie(
        of_core, far_side, near_far, mine[1], local[2]
    )
    near[0] = (*near_own, *near_far)
    far_other, near_own = spread_high(mine[1], 1), spread_low(mine[1:2])
    mine[2] = paired(*local[2])
    column_pieces = [[row, [hop(piece, 0, 1) for piece in row]] for row in of_core]
    column_at = jnp.stack([head ^ (2 * y + c) for c in range(2) for y in range(ys)])
    normed_in, embedded_own = joined_norm(column_pieces, column_at, gains_full[0], own)
    w_first = assembled(mine[0], far[0], near[0], 60)
    head_columns = w_first.shape[-1] // 4
    w_in, w_out = w_first[:, : 3 * head_columns], w_first[:, 3 * head_columns :]
    local_heads = head_columns // HD
    mixed = dot(normed_in, w_in, ((1,), (0,)), HALF)
    mixed, near_own, far_other, mine[2], local[3] = tie(
        mixed, near_own, far_other, mine[2], local[3]
    )
    mine[3] = paired(*local[3])
    far[1] = both_sides(far_side, far_other)
    far_side = spread_high(mine[2], 0)
    block_order = (
        ((core ^ jnp.arange(2))[:, None, None] * 2 + (side ^ jnp.arange(2))[None, :, None]) * ys
        + (y_at ^ jnp.arange(ys))[None, None]
    ).reshape(-1)
    query_pos = place * team + (block_order[:, None] * own + jnp.arange(own)[None]).reshape(-1)
    query_pos = query_pos.astype(jnp.int32)

    def key_pos(back):
        return jnp.where(query_pos >= back * team, query_pos - back * team, length)

    pairs_own = mixed[:, head_columns:]
    earlier = [lax.ppermute(pairs_own, "blk", index_of(back)) for back in range(1, per_clip)]
    running = attend(
        mixed, mixed, local_heads, query_pos, query_pos, (), per_clip == 1, local_heads
    )
    running, earlier, far_side, far[1], mine[2], mine[3] = tie(
        running, earlier, far_side, far[1], mine[2], mine[3]
    )
    far_other, near_far = spread_high(mine[2], 1), spread_low(far[1])
    for back in range(1, per_clip):
        running = attend(
            mixed,
            earlier[back - 1],
            0,
            query_pos,
            key_pos(back),
            running,
            back == per_clip - 1,
            local_heads,
        )
    flat_heads, log_total = running
    made = core_sum(flat_heads[:half], flat_heads[half:], w_out, ((1,), (1,)))
    made, mine[2] = tie(made, mine[2])
    near_next = spread_low(mine[2:3])
    first, near_far, far_other = group_sum(made, near_far, far_other)
    near[1] = (*near_own, *near_far)
    w_up = assembled(mine[1], far[1], near[1])
    first = embedded_own + first
    far[2] = both_sides(far_side, far_other)
    far_side, near_far = spread_high(mine[3], 0), spread_low(far[2])
    normed_mid, far_side, near_far, near_next, w_up, mine[3] = gathered(
        rms_norm(first, gains_full[1]).astype(HALF), far_side, near_far, near_next, w_up, mine[3]
    )
    near[2] = (*near_next, *near_far)
    w_down = assembled(mine[2], far[2], near[2])
    hidden_up = [dot(part, w_up, ((1,), (0,))) for part in normed_mid]
    active = [jax.nn.gelu(part).astype(HALF) for part in hidden_up]
    near_own, far_other = spread_low(mine[3:]), spread_high(mine[3], 1)
    made = core_sum(*active, w_down, ((1,), (1,)))
    second, near_own, far_other = group_sum(made, near_own, far_other)
    far[3] = both_sides(far_side, far_other)
    second = first + second
    final_in, *near_far = gathered(
        rms_norm(second, gains_full[2]).astype(HALF), *spread_low(far[3])
    )
    w_read = assembled(mine[3], far[3], (*near_own, *near_far))
    logits = [dot(part, w_read, ((1,), (0,))) for part in final_in]

    def of_team(array):
        taken = lax.dynamic_slice(array, (clip, place * team), (1, team))
        return taken.reshape(ranks, own)[block_order].reshape(team)

    weight_all = (
        (mask_all == 1) & (jnp.arange(length)[None, :] < clip_lengths[:, None])
    ).astype(F32)
    loss_count = jnp.sum(weight_all)
    weight_of = of_team(weight_all)
    targets_own = of_team(targets_all)
    vocab_local = logits[0].shape[1]
    column_ids = (head * 2 + side) * vocab_local + jnp.arange(vocab_local)
    halves = (slice(0, half), slice(half, team))
    match = [column_ids[None, :] == targets_own[at][:, None] for at in halves]
    parts = []
    for part, hit in zip(logits, match):
        top = jnp.max(part, axis=-1)
        total = jnp.sum(jnp.exp(part - top[:, None]), axis=-1)
        parts.append(jnp.stack([top, total, jnp.sum(jnp.where(hit, part, 0.0), axis=-1)]))
    stats = jnp.concatenate(parts, axis=1)
    for axis, bits in [(2, (PAIR, 0)), (1, (0, 1))] + [
        (3, (0, 2 << k)) for k in range(ys.bit_length() - 1)
    ]:
        other = hop(stats, *bits).reshape(3, 2, 2, ys, own)
        flipped = np.arange(other.shape[axis]) ^ (bits[1] // 2 if axis == 3 else 1)
        other = jnp.stack(
            [lax.index_in_dim(other, k, axis, keepdims=False) for k in flipped], axis=axis
        ).reshape(3, team)
        top = jnp.maximum(stats[0], other[0])
        total = stats[1] * jnp.exp(stats[0] - top) + other[1] * jnp.exp(other[0] - top)
        stats = jnp.stack([top, total, stats[2] + other[2]])
    log_norm = stats[0] + jnp.log(stats[1])
    per_token = (log_norm + ZCOEF * log_norm * log_norm - stats[2]) * weight_of
    loss_part = jnp.sum(per_token) * (rank == 0).astype(F32)

    token_grad = weight_of / loss_count
    grad_logits = []
    for part, hit, at in zip(logits, match, halves):
        probs = jnp.exp(part - log_norm[at][:, None])
        scaled = probs * (1.0 + 2.0 * ZCOEF * log_norm[at])[:, None] - hit.astype(F32)
        grad_logits.append((token_grad[at][:, None] * scaled).astype(HALF))

    top_bit = high_bits[-1]
    top = (blk // top_bit) % 2

    def made_of(left, right):
        return dot(left, right, ((0,), (0,)), HALF).reshape(
            2, highs // 2, 2, 2, rows, right.shape[1]
        )

    def low_part(made, at_top, at_low):
        chosen = lax.dynamic_index_in_dim(made, at_top, 0, keepdims=False)
        return lax.dynamic_index_in_dim(chosen, at_low, 2, keepdims=False)

    def send_low(made, at_top):
        return flip(low_part(made, at_top, 1 - low), 1)

    def add_low(made, at_top, came):
        return low_part(made, at_top, low).astype(F32) + came.astype(F32)

    def for_top(made, came):
        total = add_low(made, 1 - top, came).astype(HALF)
        return total[:, 0], total[:, 1]

    def send_high(part):
        return flip(part, top_bit)

    def add_high(made, came_low, came_high):
        total = add_low(made, top, came_low) + jnp.stack(came_high, axis=1).astype(F32)
        total = total.reshape((2,) * (len(high_bits) - 1) + total.shape[1:])
        for bit in high_bits[-2::-1] if len(high_bits) > 1 else []:
            at = (blk // bit) % 2
            send = lax.dynamic_index_in_dim(total, 1 - at, 0, keepdims=False)
            keep = lax.dynamic_index_in_dim(total, at, 0, keepdims=False)
            total = keep + flip(send.astype(HALF), bit).astype(F32)
        return total

    def sum_sides(total):
        send = lax.dynamic_index_in_dim(total, 1 - side, 0, keepdims=False)
        keep = lax.dynamic_index_in_dim(total, side, 0, keepdims=False)
        came = flip(send.astype(HALF), PAIR).astype(F32)
        return jnp.where(side == 0, keep, came), jnp.where(side == 0, came, keep)

    def joined(parts):
        return jnp.concatenate(parts)

    made = core_sum(*grad_logits, w_read, ((1,), (1,)))
    made, read_made = tie(made, made_of(joined(final_in), joined(grad_logits)))
    read_far = send_low(read_made, 1 - top)
    grad_final, read_made, read_far = group_sum(made, read_made, read_far)
    read_near = send_low(read_made, top)
    read_top = for_top(read_made, read_far)
    read_first = send_high(read_top[0])
    grad_second, gain_final = norm_back(second, gains_full[2], grad_final)
    branch_grad, read_near, read_first, read_top = gathered(
        grad_second.astype(HALF), read_near, read_first, read_top
    )
    read_second = send_high(read_top[1])
    grad_hidden = []
    for part, up in zip(branch_grad, hidden_up):
        unused_gelu, gelu_pull = jax.vjp(jax.nn.gelu, up)
        grad_hidden.append(gelu_pull(dot(part, w_down, ((1,), (0,))))[0].astype(HALF))
    made = core_sum(*grad_hidden, w_up, ((1,), (1,)))
    made, normed_mid, grad_hidden, read_second, down_made = tie(
        made,
        normed_mid,
        grad_hidden,
        read_second,
        made_of(joined(branch_grad), joined(active)),
    )
    read_total = add_high(read_made, read_near, (read_first, read_second))
    down_far = send_low(down_made, 1 - top)
    grad_mid, down_made, down_far, up_made = group_sum(
        made, down_made, down_far, made_of(joined(normed_mid), joined(grad_hidden))
    )
    down_near = send_low(down_made, top)
    down_top = for_top(down_made, down_far)
    down_first = send_high(down_top[0])
    grad_mid_in, gain_mid = norm_back(first, gains_full[1], grad_mid)
    grad_first = grad_second + grad_mid_in
    attn_grad, up_made, down_near, down_first, down_top, read_total = gathered(
        grad_first.astype(HALF), up_made, down_near, down_first, down_top, read_total
    )
    down_second = send_high(down_top[1])
    up_far = send_low(up_made, 1 - top)
    attn_grad = joined(attn_grad)
    grad_heads = dot(attn_grad, w_out, ((1,), (0,)), HALF)
    returned = []
    grad_query = None
    for back in range(1, per_clip):
        grad_query, far_pairs = attend_back(
            mixed,
            earlier[back - 1],
            0,
            query_pos,
            key_pos(back),
            flat_heads,
            grad_heads,
            log_total,
            grad_query,
            False,
            local_heads,
        )
        if back == 1:
            far_pairs, up_made, up_far, down_second, read_total = tie(
                far_pairs, up_made, up_far, down_second, read_total
            )
            grad_read = sum_sides(read_total)
            grad_down = sum_sides(add_high(down_made, down_near, (down_first, down_second)))
            up_near = send_low(up_made, top)
            up_top = for_top(up_made, up_far)
            up_first = send_high(up_top[0])
        returned.append(lax.ppermute(far_pairs, "blk", index_of(-back)))
    grad_query, grad_pairs = attend_back(
        mixed,
        mixed,
        local_heads,
        query_pos,
        query_pos,
        flat_heads,
        grad_heads,
        log_total,
        grad_query,
        True,
        local_heads,
    )
    for far_pairs in returned:
        grad_pairs = grad_pairs + far_pairs.astype(F32)
    grad_mixed = jnp.concatenate([grad_query, grad_pairs.astype(HALF)], axis=1)
    grad_mixed, up_first, up_top, grad_read = tie(grad_mixed, up_first, up_top, grad_read)
    up_second = send_high(up_top[1])
    made = core_sum(grad_mixed[:half], grad_mixed[half:], w_in, ((1,), (1,)))
    made, in_made, out_made, grad_down = tie(
        made, made_of(normed_in, grad_mixed), made_of(attn_grad, flat_heads), grad_down
    )
    grad_norm_in, in_made, out_made, up_near, up_second = group_sum(
        made, in_made, out_made, up_near, up_second
    )
    in_far, out_far = send_low(in_made, 1 - top), send_low(out_made, 1 - top)
    grad_embed_in, gain_in = norm_back(embedded_own, gains_full[0], grad_norm_in)
    grad_embed = (grad_first + grad_embed_in).astype(HALF)

    def columns_of(head_bits):
        at = (head ^ head_bits) * width
        return lax.dynamic_slice(grad_embed, (0, at), (own, width))

    head_bits = [2 * y + c for c in range(2) for y in range(ys)]
    head_parts = [
        columns_of(bits) if bits == 0 else hop(columns_of(bits), 0, bits) for bits in head_bits
    ]
    grad_up = sum_sides(add_high(up_made, up_near, (up_first, up_second)))
    head_parts, in_made, out_made, in_far, out_far = tie(
        head_parts, in_made, out_made, in_far, out_far
    )
    in_near, out_near = send_low(in_made, top), send_low(out_made, top)
    in_top, out_top = for_top(in_made, in_far), for_top(out_made, out_far)
    in_first, out_first = send_high(in_top[0]), send_high(out_top[0])
    columns_own = jnp.concatenate(head_parts)
    gain_own = jnp.stack([gain_in, gain_mid, gain_final])
    for k in range(heads.bit_length() - 1):
        gain_own = gain_own + hop(gain_own, 0, 1 << k)

    def spread(pieces, bit):
        return jnp.concatenate([pieces, flip(pieces, bit)])

    mid = width // 2
    gain_rows = gain_own.astype(HALF).reshape(-1, width - mid)
    gain_rows = jnp.pad(gain_rows, ((0, -gain_rows.shape[0] % 16), (0, 0)))
    pieces_a, pieces_b = tie(
        columns_own[None, :, :mid], jnp.concatenate([columns_own[:, mid:], gain_rows])[None]
    )
    for bit in high_bits[::-1]:
        pieces_a, pieces_b = spread(pieces_a, bit), spread(pieces_b, bit)
    pieces_a, pieces_b, in_first, out_first, in_top, out_top, in_near, out_near = tie(
        pieces_a, pieces_b, in_first, out_first, in_top, out_top, in_near, out_near
    )
    in_second, out_second = send_high(in_top[1]), send_high(out_top[1])
    pieces_a, pieces_b = spread(pieces_a, PAIR), spread(pieces_b, 1)
    pieces_a, pieces_b, in_second, out_second, grad_up = tie(
        pieces_a, pieces_b, in_second, out_second, grad_up
    )
    pieces = (pieces_a, flip(pieces_a, 1), pieces_b, flip(pieces_b, PAIR))
    pieces, in_total, out_total = tie(
        pieces,
        add_high(in_made, in_near, (in_first, in_second)),
        add_high(out_made, out_near, (out_first, out_second)),
    )
    grad_in, grad_out_w = sum_sides(in_total), sum_sides(out_total)
    gain_sum = sum(jnp.sum(part[:, half:].astype(F32), axis=0) for part in pieces[2:])
    gain_sum = gain_sum.reshape(-1)[: 3 * D].reshape(3, D)
    gain_sum = lax.dynamic_slice_in_dim(gain_sum, blk * rows, rows, 1)
    masks_a, masks_b = [0], [0]
    for bit_a, bit_b in zip(high_bits[::-1] + [PAIR, 1], high_bits[::-1] + [1, PAIR]):
        masks_a = masks_a + [mask | bit_a for mask in masks_a]
        masks_b = masks_b + [mask | bit_b for mask in masks_b]
    places = [[masks.index(mask) for mask in range(blocks)] for masks in (masks_a, masks_b)]
    row_step = max(s for s in range(8, 321, 8) if table_rows % s == 0)
    grad_table = table_grad(table_at, pieces, places, table_rows, row_step)
    img_sum, code_sum = grad_table[:image_rows], grad_table[image_rows:]

    in_sum = jnp.stack(
        [
            jnp.concatenate(
                [part[:, k * head_columns : (k + 1) * head_columns] for part in grad_in], axis=1
            )
            for k in range(3)
        ]
    )
    out_sum = jnp.concatenate([part.T for part in grad_out_w])
    down_sum = jnp.concatenate([part.T for part in grad_down])
    up_sum = jnp.concatenate(grad_up, axis=1)
    read_sum = jnp.concatenate(grad_read, axis=1)
    in_sum, out_sum, up_sum, down_sum, read_sum = (
        with_layout_constraint(total, Layout(major_to_minor=tuple(range(total.ndim))))
        for total in (in_sum, out_sum, up_sum, down_sum, read_sum)
    )
    sums = [in_sum, out_sum, up_sum, down_sum, img_sum, code_sum, read_sum, gain_sum]
    local_squares = jnp.float32(0.0)
    for shard in sums[:7]:
        local_squares = local_squares + jnp.sum(shard * shard)
    local_squares = local_squares + (head == 0).astype(F32) * jnp.sum(gain_sum * gain_sum)
    mine = jnp.broadcast_to(
        jnp.stack([local_squares, loss_part])[None, :, None], (blocks * heads, 2, 128)
    )
    totals = jnp.sum(lax.all_to_all(mine, both, 0, 0, tiled=True), axis=0)
    grad_norm = jnp.sqrt(totals[0, 0])
    loss_sum = totals[1, 0]
    factor = jnp.minimum(1.0, CLIP / grad_norm)
    spreads = [
        D ** (-0.5),
        (length // 2) ** 0.5 * D ** (-0.5),
        D ** (-0.5),
        FF ** (-0.5),
        0.05,
        0.05,
        2.0 * D ** (-0.5),
    ]
    weights = [inward, outward, expand, contract, image_table, code_table, readout, gains]
    firsts = [
        inward_first,
        outward_first,
        expand_first,
        contract_first,
        image_first,
        code_first,
        readout_first,
        gains_first,
    ]
    seconds = [
        inward_second,
        outward_second,
        expand_second,
        contract_second,
        image_second,
        code_second,
        readout_second,
        gains_second,
    ]
    result = []
    for index in range(8):
        rate = GAIN_RATE if index == 7 else RATE_FACTOR * spreads[index]
        decay = 0.0 if index == 7 else DECAY
        result.extend(
            adamw(weights[index], firsts[index], seconds[index], sums[index] * factor, rate, decay)
        )
    return (*result, loss_sum, loss_count, grad_norm)


def solution(mesh):
    matrices = (
        P(None, "blk", "head"),
        P("head", "blk"),
        P("blk", "head"),
        P("head", "blk"),
        P("blk", "head"),
        P("blk", "head"),
        P("blk", "head"),
        P(None, "blk"),
    )
    tokens = P(None, "blk")
    return jax.shard_map(
        shards,
        mesh=mesh,
        in_specs=matrices * 3 + (tokens, tokens, P(), tokens, tokens),
        out_specs=tuple(spec for spec in matrices for _ in range(3)) + (P(), P(), P()),
        check_vma=False,
    )
```
